512 devices in a mesh: tile: 128 (over y, z, core), chan: 4 (over x).
Axes of the slice: x: 4, y: 4, z: 16, core: 2. Of those that a mesh axis runs over, the one named last changes fastest.
Arguments:
- spectra: float32 [16384, 4096], P('tile', 'chan'), as said below
- feed_ids: int32 [16384], P('tile'), may hold values from 0 to 18
- feed_gain: float32 [19, 4096], P(None, 'chan'), may hold values from 0.1 to 1.9
- send_list: int32 [1024, 64], P('tile'), may hold values from 0 to 127, as said below
- send_count: int32 [1024], P('tile'), may hold values from 0 to 64, as said below
- kernel_weight: float32 [65536, 64], P('tile'), may hold values from 0 to 1.5
- pixel_block: int32 [65536], P('tile'), may hold values from 0 to 3
- beam_width: float32 [4096], P(('chan', 'tile')), may hold values from 1.5 to 12
Outputs:
- smoothed: float32 [4096, 256, 128], P(('chan', 'tile'))
The draws below stay inside these ranges and needn't reach their ends.
Inputs may be any that keep to these rules, and one draw needn't show every extreme that they name: `send_count`: entry s * 8 + o is the number of samples that slab s sends to tile (s + o - 4) mod 128; in every draw some tile receives 64 from each of the 8 slabs that send to it. `send_list`: the 64 entries of a row are distinct. Positive spectra.
All inputs are finite; a program needn't handle non-finite values.
Results may differ from the reference program's by a relative error of at most 0.0003.
Values sent between devices are 32-bit elements; how exact they have to be, the bound alone decides.
No kernel may reach another device: no remote copies, remote signals or barrier semaphores. Data moves between devices by JAX's collectives and lax.ppermute only.
A program may use at most 64 MiB of HBM per device.

```python
import math
import jax
import jax.numpy as jnp
from jax import lax

CH = 4096
FEEDS = 19
S_DEV = 128
BAND = 8
TY = 2
TX = 128
KB = 64
HALF = 4
CAP = 64
TILES = 128
SAMPLES = 16384
SLOTS = 512
PIX = 256
NBLK = 4
NROW = 256


def draw_spectra(key, part):
    key = jax.random.fold_in(key, 11)
    first, second = jax.random.split(key, 2)
    channel = jnp.arange(CH, dtype=jnp.float32) / CH
    level = jnp.exp(jax.random.uniform(first, (SAMPLES, 1), minval=math.log(0.5), maxval=math.log(5.0)))
    bandpass = 1.0 + 4.0 * channel
    ripple = jax.random.uniform(second, (SAMPLES, CH), minval=-1.0, maxval=1.0)
    return (level * bandpass[None, :] * (1.0 + 0.3 * ripple)).astype(jnp.float32)


def draw_send_list(key, part):
    key = jax.random.fold_in(key, 14)
    scores = jax.random.randint(key, (TILES * BAND, S_DEV), 0, 1 << 18) * S_DEV
    scores = scores + jnp.arange(S_DEV, dtype=jnp.int32)[None, :]
    ordering = jnp.argsort(scores, axis=1)
    return ordering[:, :CAP].astype(jnp.int32)


def draw_send_count(key, part):
    key = jax.random.fold_in(key, 12)
    first, second = jax.random.split(key, 2)
    counts = jax.random.randint(first, (TILES, BAND), 0, CAP + 1)
    filled = jax.random.randint(second, (), 0, TILES)
    slab_index = jnp.arange(TILES, dtype=jnp.int32)[:, None]
    band_offset = jnp.arange(BAND, dtype=jnp.int32)[None, :]
    target = (slab_index + band_offset - HALF) % TILES
    counts = jnp.where(target == filled, CAP, counts)
    return counts.reshape(-1).astype(jnp.int32)


def draw_kernel_weight(key, part):
    key = jax.random.fold_in(key, 13)
    first, second, third = jax.random.split(key, 3)
    total_rows = TILES * SLOTS
    center = jax.random.uniform(first, (total_rows, 1), minval=0.25 * KB, maxval=0.75 * KB)
    spread = KB * jnp.exp(jax.random.uniform(second, (total_rows, 1), minval=math.log(0.025), maxval=math.log(0.1)))
    rough = jax.random.uniform(third, (total_rows, KB), minval=0.5, maxval=1.5)
    position = jnp.arange(KB, dtype=jnp.float32)[None, :]
    return (jnp.exp(-(position - center) ** 2 / (2.0 * spread ** 2)) * rough).astype(jnp.float32)


def set_ends(drawn, stream_key, smallest, top_value):
    spot = [jax.random.randint(jax.random.fold_in(stream_key, axis), (), 0, length) for axis, length in enumerate(drawn.shape)]
    main_axis = drawn.shape.index(max(drawn.shape))
    beside = spot[:main_axis] + [(spot[main_axis] + 1) % drawn.shape[main_axis]] + spot[main_axis + 1:]
    return drawn.at[tuple(spot)].set(smallest).at[tuple(beside)].set(top_value)


def steps_of(rng, extent, cuts, least, top_value):
    def one(axis_at, blocks):
        draws = jax.random.uniform(jax.random.fold_in(jax.random.fold_in(rng, 6), axis_at), (blocks,), jnp.float32, least / len(cuts), top_value / len(cuts))
        return jnp.repeat(jnp.exp(draws), extent[axis_at] // blocks).reshape((-1,) + (1,) * (len(extent) - axis_at - 1))

    loudness = one(*cuts[0])
    for cut in cuts[1:]:
        loudness = loudness * one(*cut)
    return loudness


def setup_inputs(seed: int = 0) -> dict:
    seeds = jax.random.split(jax.random.key(seed), 9)
    return {
        "spectra": draw_spectra(jax.random.fold_in(seeds[8], 71), 0),
        "feed_ids": set_ends(jax.random.randint(seeds[1], (SAMPLES,), 0, FEEDS), jax.random.fold_in(seeds[1], 1), 0, FEEDS - 1).astype(jnp.int32),
        "feed_gain": jnp.clip(1.0 + 0.18 * jax.random.normal(seeds[2], (FEEDS, CH), jnp.float32), 0.1, 1.9),
        "send_list": draw_send_list(jax.random.fold_in(seeds[8], 71), 0),
        "send_count": draw_send_count(jax.random.fold_in(seeds[8], 71), 0),
        "kernel_weight": draw_kernel_weight(jax.random.fold_in(seeds[8], 71), 0),
        "pixel_block": set_ends(jax.random.randint(seeds[6], (TILES * SLOTS,), 0, NBLK), jax.random.fold_in(seeds[6], 1), 0, NBLK - 1).astype(jnp.int32),
        "beam_width": jnp.clip(jnp.exp(math.log(12.0) - 2.0794415 * jax.random.uniform(seeds[7], (CH,), jnp.float32) ** steps_of(seeds[7], (CH,), ((0, 512),), -0.2, 0.2)), 1.5, 12.0),
    }


highest = lax.Precision.HIGHEST


def circular_response(beam_sigma, length):
    frequency = jnp.arange(length, dtype=jnp.int32)
    folded = jnp.minimum(frequency, length - frequency).astype(jnp.float32) / length
    return jnp.exp(-2.0 * math.pi ** 2 * beam_sigma[:, None] ** 2 * folded[None, :] ** 2)


def reference(spectra, feed_ids, feed_gain, send_list, send_count, kernel_weight, pixel_block, beam_width):
    onehot = (feed_ids[:, None] == jnp.arange(FEEDS, dtype=jnp.int32)[None, :]).astype(jnp.float32)
    gain_rows = jnp.dot(onehot, feed_gain, precision=highest)
    band_mean = jnp.sum(spectra, axis=1) / CH
    calibrated = gain_rows * spectra / band_mean[:, None]
    lists = send_list.reshape(TILES, BAND, CAP)
    counts = send_count.reshape(TILES, BAND)
    band_offsets = jnp.arange(BAND, dtype=jnp.int32)
    slot_index = jnp.arange(CAP, dtype=jnp.int32)
    block_index = jnp.arange(NBLK, dtype=jnp.int32)

    def grid_tile(owner):
        senders = (owner - band_offsets + HALF) % TILES
        chosen = lists[senders, band_offsets, :]
        row_index = (senders[:, None] * S_DEV + chosen).reshape(-1)
        live_mask = (slot_index[None, :] < counts[senders, band_offsets][:, None]).reshape(-1).astype(jnp.float32)
        spectra_block = calibrated[row_index]
        start = (owner * SLOTS).astype(jnp.int32)
        weights = lax.dynamic_slice_in_dim(kernel_weight, start, SLOTS, 0) * live_mask[:, None]
        blocks_of = lax.dynamic_slice_in_dim(pixel_block, start, SLOTS, 0)
        selector = (blocks_of[None, :] == block_index[:, None]).astype(jnp.float32)
        dense_weights = (selector[:, None, :] * weights.T[None, :, :]).reshape(PIX, SLOTS)
        numerator = jnp.dot(dense_weights, spectra_block, precision=highest)
        weight_sum = jnp.sum(dense_weights, axis=1)
        return numerator / jnp.maximum(weight_sum, 1.0)[:, None]

    gridded = lax.map(grid_tile, jnp.arange(TILES, dtype=jnp.int32))
    field = gridded.reshape(TILES, TY, TX, CH).transpose(3, 0, 1, 2).reshape(CH, NROW, TX)
    row_response = circular_response(beam_width, NROW)
    column_response = circular_response(beam_width, TX)
    group = 16

    def smooth(items):
        sky_image, rows_h, columns_h = items
        transform = jnp.fft.fft2(sky_image)
        filtered = transform * rows_h[:, :, None] * columns_h[:, None, :]
        return jnp.real(jnp.fft.ifft2(filtered)).astype(jnp.float32)

    smoothed = lax.map(smooth, (field.reshape(CH // group, group, NROW, TX),
                                row_response.reshape(CH // group, group, NROW),
                                column_response.reshape(CH // group, group, TX)))
    return smoothed.reshape(CH, NROW, TX)
```

```python
import math

import jax
import jax.numpy as jnp
from jax import lax
from jax.experimental import pallas as pl
from jax.experimental.pallas import tpu as pltpu
from jax.sharding import Mesh
from jax.sharding import PartitionSpec as P

CH = 4096
TY = 2
TX = 128
CORES = 2
ROWS_Z = 16
SLAB = 128
BAND = 8
CAP = 64
KB = 64
HALF_CH = 512
META = 8
UNIT = HALF_CH + META
REACH = 9
PIX = TY * TX

f32 = jnp.float32
bf16 = jnp.bfloat16
highest = lax.Precision.HIGHEST
VMEM = pltpu.VMEM


def whole(memory_space=VMEM):
    return pl.BlockSpec(memory_space=memory_space)


def split(value):
    high = value.astype(bf16)
    return high, (value - high.astype(f32)).astype(bf16)


def prepare_kernel(
    spectra, feed_ids, feed_gain, send_list, counts, weights, blocks, unit, packed, gains
):
    feeds = feed_gain.shape[0]
    gains[...] = jnp.zeros_like(gains)
    gains[0:feeds, :] = feed_gain[...]
    onehot = (
        lax.broadcasted_iota(jnp.int32, (gains.shape[0], SLAB), 0) == feed_ids[...]
    ).astype(f32)
    gain_rows = lax.dot_general(
        gains[...], onehot, (((0,), (0,)), ((), ())), precision=highest, preferred_element_type=f32
    )
    raw = spectra[...].T
    band_sum = jnp.sum(raw, axis=0, keepdims=True)
    scaled = (raw * gain_rows).reshape(HALF_CH // 8, CORES, 8, SLAB)
    lane = lax.broadcasted_iota(jnp.int32, (1, CAP), 1)
    rows = []
    for row in range(BAND):
        rows.append(
            jnp.where(lane < counts[row], send_list[row : row + 1, :], -1).astype(f32)
        )
    rows = [jnp.concatenate(rows[2 * m : 2 * m + 2], axis=1) for m in range(BAND // 2)]
    meta = jnp.concatenate(rows + [band_sum, jnp.zeros((META - BAND // 2 - 1, SLAB), f32)], axis=0)
    for core in range(CORES):
        unit[core, 0:HALF_CH, :] = scaled[:, core].reshape(HALF_CH, SLAB)
        unit[core, HALF_CH:UNIT, :] = meta
    wide = jnp.concatenate([weights[...], jnp.zeros((BAND * CAP, KB), f32)], axis=1)
    packed[0:KB, :] = wide.T[0:KB, :]
    packed[KB : KB + 8, :] = jnp.broadcast_to(blocks[...].astype(f32), (8, BAND * CAP))


def prepare(spectra, feed_ids, feed_gain, send_list, send_count, kernel_weight, pixel_block):
    slots = BAND * CAP
    return pl.pallas_call(
        prepare_kernel,
        out_shape=(
            jax.ShapeDtypeStruct((CORES, UNIT, SLAB), f32),
            jax.ShapeDtypeStruct((KB + 8, slots), f32),
        ),
        in_specs=[
            whole(),
            whole(),
            whole(),
            whole(),
            whole(pltpu.SMEM),
            whole(),
            whole(),
        ],
        out_specs=(whole(), whole()),
        scratch_shapes=[VMEM((24, spectra.shape[1]), f32)],
        compiler_params=pltpu.CompilerParams(vmem_limit_bytes=24 << 20),
        name="prepare",
    )(
        spectra,
        feed_ids.reshape(1, SLAB),
        feed_gain,
        send_list,
        send_count,
        kernel_weight,
        pixel_block.reshape(1, slots),
    )


def grid_kernel(
    core, below2, below1, here, above1, above2, sum_b2, sum_b1, sum_h, sum_a1, sum_a2,
    packed_own, packed_other, out, left, right, dense,
):
    me = core[0]
    for tile in range(CORES):
        pack = jnp.where(me == tile, packed_own[...], packed_other[...])
        weight = pack[0:KB, :]
        block = pack[KB : KB + 1, :]
        for number in range(PIX // KB):
            high, low = split(jnp.where(block == number, weight, 0.0))
            dense[tile, number * KB : (number + 1) * KB, :] = high
            dense[tile, PIX + number * KB : PIX + (number + 1) * KB, :] = low
    slabs = [
        (below2, None, sum_b2, 0),
        (below1, 0, sum_b1, 0),
        (below1, 1, sum_b1, 1),
        (here, 0, sum_h, 0),
        (here, 1, sum_h, 1),
        (above1, 0, sum_a1, 0),
        (above1, 1, sum_a1, 1),
        (above2, 0, sum_a2, 0),
        (above2, 1, sum_a2, 1),
    ]
    depth = REACH * SLAB
    totals = [jnp.zeros((1, PIX), f32) for _ in range(CORES)]
    sample = lax.broadcasted_iota(jnp.int32, (SLAB, SLAB), 0).astype(f32)
    lane = lax.broadcasted_iota(jnp.int32, (SLAB, SLAB), 1)
    for index, (ref, part, sums, row) in enumerate(slabs):
        unit = ref if part is None else ref.at[part]
        scale = CH / sums[row : row + 1, :]
        high, low = split(unit[0:HALF_CH, :] * scale)
        at = index * SLAB
        left[:, at : at + SLAB] = high
        left[:, depth + at : depth + at + SLAB] = low
        left[:, 2 * depth + at : 2 * depth + at + SLAB] = high
        for tile in range(CORES):
            offset = tile + BAND - 1 - index
            columns = slice(tile * PIX, (tile + 1) * PIX)
            if not 0 <= offset < BAND:
                for copy in range(3):
                    start = copy * depth + at
                    right[start : start + SLAB, columns] = jnp.zeros((SLAB, PIX), bf16)
                continue
            pair = offset // 2
            chosen = unit[HALF_CH + pair : HALF_CH + pair + 1, :]
            hot = ((sample == chosen) & ((lane // CAP) == offset % 2)).astype(f32).astype(bf16)
            picked = lax.dot_general(
                hot,
                dense[tile, :, pair * SLAB : (pair + 1) * SLAB],
                (((1,), (1,)), ((), ())),
                preferred_element_type=f32,
            )
            top, rest = picked[:, 0:PIX], picked[:, PIX:]
            totals[tile] = totals[tile] + jnp.sum(top + rest, axis=0, keepdims=True)
            top, rest = top.astype(bf16), rest.astype(bf16)
            right[at : at + SLAB, columns] = top
            right[depth + at : depth + at + SLAB, columns] = top
            right[2 * depth + at : 2 * depth + at + SLAB, columns] = rest
    total = jnp.maximum(jnp.concatenate(totals, axis=1), 1.0)
    tiles = jnp.dot(left[...], right[...], preferred_element_type=f32) / total
    for row in range(CORES * TY):
        out[:, row] = tiles[:, row * TX : (row + 1) * TX].reshape(HALF_CH // 8, 8, TX)


def grid_tiles(core, units, sums, packed_own, packed_other):
    slots = BAND * CAP
    depth = REACH * SLAB
    return pl.pallas_call(
        grid_kernel,
        out_shape=jax.ShapeDtypeStruct((HALF_CH // 8, CORES * TY, 8, TX), f32),
        in_specs=[whole(pltpu.SMEM)] + [whole()] * 12,
        out_specs=whole(),
        scratch_shapes=[
            VMEM((HALF_CH, 3 * depth), bf16),
            VMEM((3 * depth, CORES * PIX), bf16),
            VMEM((CORES, 2 * PIX, slots), bf16),
        ],
        compiler_params=pltpu.CompilerParams(vmem_limit_bytes=32 << 20),
        name="grid_tiles",
    )(core, *units, *sums, packed_own, packed_other)


def waves(length):
    frequency = jnp.arange(length, dtype=jnp.int32)
    phases = (frequency[:, None] * frequency[None, :] % length).astype(f32) * (
        2.0 * math.pi / length
    )
    return jnp.concatenate([jnp.cos(phases), jnp.sin(phases)], axis=1)


def response(sigma, length):
    frequency = lax.broadcasted_iota(jnp.int32, (1, 2 * length), 1) % length
    folded = jnp.minimum(frequency, length - frequency).astype(f32) / length
    return jnp.exp(-2.0 * math.pi**2 * sigma**2 * folded**2)


def circulant(sigma, basis):
    length = basis.shape[0]
    return (
        lax.dot_general(
            basis * response(sigma, length),
            basis,
            (((1,), (1,)), ((), ())),
            precision=highest,
            preferred_element_type=f32,
        )
        / length
    )


def tables_kernel(sigma, row_waves, column_waves, rows_out, columns_out):
    width = sigma[pl.program_id(0)]
    high, low = split(circulant(width, row_waves[...]))
    size = high.shape[0]
    rows_out[0, :, 0:size] = high
    rows_out[0, :, size : 2 * size] = high
    rows_out[0, :, 2 * size : 3 * size] = low
    high, low = split(circulant(width, column_waves[...]))
    columns_out[0, 0:TX, :] = high
    columns_out[0, TX : 2 * TX, :] = high
    columns_out[0, 2 * TX : 3 * TX, :] = low


def make_tables(sigma, length):
    channels = sigma.shape[0]
    waves_rows = waves(length)
    fixed = lambda shape: pl.BlockSpec(shape, lambda c: (0, 0))
    return pl.pallas_call(
        tables_kernel,
        grid=(channels,),
        out_shape=(
            jax.ShapeDtypeStruct((channels, length, 3 * length), bf16),
            jax.ShapeDtypeStruct((channels, 3 * TX, TX), bf16),
        ),
        in_specs=[
            whole(pltpu.SMEM),
            fixed((length, 2 * length)),
            fixed((TX, 2 * TX)),
        ],
        out_specs=(
            pl.BlockSpec((1, length, 3 * length), lambda c: (c, 0, 0)),
            pl.BlockSpec((1, 3 * TX, TX), lambda c: (c, 0, 0)),
        ),
        compiler_params=pltpu.CompilerParams(vmem_limit_bytes=16 << 20),
        cost_estimate=pl.CostEstimate(
            flops=2 * channels * 6 * 2 * length**3, bytes_accessed=6 << 20, transcendentals=0
        ),
        name="smoothing_tables",
    )(sigma, waves_rows, waves(TX))


def smooth_kernel(field, rows_table, columns_table, out):
    channel = pl.program_id(0)
    high, low = split(field[pl.ds(channel, field.shape[0] // 8, stride=8), :])
    across = jnp.dot(
        jnp.concatenate([high, low, high], axis=1), columns_table[0], preferred_element_type=f32
    )
    high, low = split(across)
    out[0] = jnp.dot(
        rows_table[0], jnp.concatenate([high, low, high], axis=0), preferred_element_type=f32
    )


def smooth(field, rows_table, columns_table):
    channels, length, _ = rows_table.shape
    return pl.pallas_call(
        smooth_kernel,
        grid=(channels,),
        out_shape=jax.ShapeDtypeStruct((channels, length, TX), f32),
        in_specs=[
            pl.BlockSpec(field.shape, lambda c: (0, 0)),
            pl.BlockSpec((1, length, 3 * length), lambda c: (c, 0, 0)),
            pl.BlockSpec((1, 3 * TX, TX), lambda c: (c, 0, 0)),
        ],
        out_specs=pl.BlockSpec((1, length, TX), lambda c: (c, 0, 0)),
        compiler_params=pltpu.CompilerParams(vmem_limit_bytes=16 << 20),
        name="smooth",
    )(field, rows_table, columns_table)


def local(
    spectra, feed_ids, feed_gain, send_list, send_count, kernel_weight, pixel_block, beam_width
):
    chips = lax.axis_size(("y", "z"))

    def shift(array, by):
        return lax.ppermute(array, ("y", "z"), [(i, (i + by) % chips) for i in range(chips)])

    unit, packed = prepare(
        spectra, feed_ids, feed_gain, send_list, send_count, kernel_weight, pixel_block
    )
    here = lax.all_to_all(unit, "core", split_axis=0, concat_axis=0, tiled=True)
    packed_other = lax.ppermute(packed, "core", [(0, 1), (1, 0)])
    above1 = shift(here, -1)
    below1 = shift(here, 1)
    above2 = shift(above1, -1)
    below2 = shift(below1[1], 1)
    sums = lax.psum(here[:, HALF_CH + BAND // 2, :], "chan")
    sum_a1, sum_b1 = shift(sums, -1), shift(sums, 1)
    sum_a2, sum_b2 = shift(sums, -2), shift(sums[1:2], 2)
    core = lax.axis_index("core").astype(jnp.int32).reshape(1)
    gridded = grid_tiles(
        core,
        (below2, below1, here, above1, above2),
        (sum_b2, sum_b1, sums, sum_a1, sum_a2),
        packed,
        packed_other,
    )
    gridded, beam_width = lax.optimization_barrier((gridded, beam_width))
    relaid = lax.all_to_all(gridded, ("y", "z"), split_axis=0, concat_axis=0, tiled=True)
    rows_table, columns_table = make_tables(beam_width, chips * CORES * TY)
    return smooth(relaid.reshape(chips * CORES * TY * 8, TX), rows_table, columns_table)


def solution(mesh):
    tiles, channels = mesh.devices.shape
    chips = tiles // CORES
    grid = Mesh(
        mesh.devices.reshape(chips // ROWS_Z, ROWS_Z, CORES, channels), ("y", "z", "core", "chan")
    )
    tile = ("y", "z", "core")
    in_specs = (
        P(tile, "chan"),
        P(tile),
        P(None, "chan"),
        P(tile, None),
        P(tile),
        P(tile, None),
        P(tile),
        P(("chan",) + tile),
    )
    out_specs = P(("chan",) + tile, None, None)
    return jax.shard_map(local, mesh=grid, in_specs=in_specs, out_specs=out_specs, check_vma=False)
```

```python
import math

import jax
import jax.numpy as jnp
from jax import lax
from jax.experimental import pallas as pl
from jax.experimental.pallas import tpu as pltpu
from jax.sharding import Mesh
from jax.sharding import PartitionSpec as P

CH = 4096
TY = 2
TX = 128
CORES = 2
ROWS_Z = 16
SLAB = 128
BAND = 8
CAP = 64
KB = 64
HALF_CH = 512
META = 8
UNIT = HALF_CH + META
TOTALS = HALF_CH + BAND // 2 + 1
REACH = 9
GROUPS = 4
VMEM_SMOOTH = 52
VMEM_PREPARE = 56
PIX = TY * TX

f32 = jnp.float32
bf16 = jnp.bfloat16
highest = lax.Precision.HIGHEST
VMEM = pltpu.VMEM


def whole(memory_space=VMEM):
    return pl.BlockSpec(memory_space=memory_space)


def split(value):
    high = value.astype(bf16)
    return high, (value - high.astype(f32)).astype(bf16)


def prepare_kernel(
    counts,
    spectra_in,
    feed_ids_in,
    feed_gain_in,
    send_list_in,
    weights_in,
    blocks_in,
    unit,
    packed,
    spectra,
    feed_ids,
    feed_gain,
    gains,
    send_list,
    blocks,
    arrived,
):
    feeds = feed_gain_in.shape[0]
    copies = []
    for source, target in (
        (feed_ids_in, feed_ids),
        (feed_gain_in, feed_gain),
        (spectra_in, spectra),
        (send_list_in, send_list),
        (blocks_in, blocks),
        (weights_in, packed.at[0:KB]),
    ):
        copies.append(pltpu.make_async_copy(source, target, arrived.at[len(copies)]))
        copies[-1].start()
    gains[...] = jnp.zeros_like(gains)
    copies[0].wait()
    copies[1].wait()
    gains[0:feeds, :] = feed_gain[...]
    onehot = (lax.broadcasted_iota(jnp.int32, (gains.shape[0], SLAB), 0) == feed_ids[...]).astype(
        f32
    )
    gain_rows = lax.dot_general(
        gains[...], onehot, (((0,), (0,)), ((), ())), precision=highest, preferred_element_type=f32
    )
    copies[2].wait()
    raw = spectra[...].T
    band_sum = jnp.sum(raw, axis=0, keepdims=True)
    scaled = (raw * gain_rows).reshape(HALF_CH // 8, CORES, 8, SLAB)
    copies[3].wait()
    lane = lax.broadcasted_iota(jnp.int32, (1, CAP), 1)
    rows = [
        jnp.where(lane < counts[row], send_list[row : row + 1, :], -1).astype(f32)
        for row in range(BAND)
    ]
    rows = [jnp.concatenate(rows[2 * m : 2 * m + 2], axis=1) for m in range(BAND // 2)]
    meta = jnp.concatenate(rows + [band_sum, jnp.zeros((META - BAND // 2 - 1, SLAB), f32)], axis=0)
    for core in range(CORES):
        unit[core, 0:HALF_CH, :] = scaled[:, core].reshape(HALF_CH, SLAB)
        unit[core, HALF_CH:UNIT, :] = meta
    copies[4].wait()
    packed[KB : KB + 8, :] = jnp.broadcast_to(blocks[...].astype(f32), (8, BAND * CAP))
    copies[5].wait()


def prepare(spectra, feed_ids, feed_gain, send_list, send_count, kernel_weight, pixel_block):
    slots = BAND * CAP
    channels = spectra.shape[1]
    return pl.pallas_call(
        prepare_kernel,
        out_shape=(
            jax.ShapeDtypeStruct((CORES, UNIT, SLAB), f32),
            jax.ShapeDtypeStruct((KB + 8, slots), f32),
        ),
        in_specs=[whole(pltpu.SMEM)] + [whole(pltpu.HBM)] * 6,
        out_specs=(whole(), whole()),
        scratch_shapes=[
            VMEM((SLAB, channels), f32),
            VMEM((1, SLAB), jnp.int32),
            VMEM(feed_gain.shape, f32),
            VMEM((24, channels), f32),
            VMEM((BAND, CAP), jnp.int32),
            VMEM((1, slots), jnp.int32),
            pltpu.SemaphoreType.DMA((6,)),
        ],
        compiler_params=pltpu.CompilerParams(vmem_limit_bytes=VMEM_PREPARE << 20),
        name="prepare",
    )(
        send_count,
        spectra,
        feed_ids.reshape(1, SLAB),
        feed_gain,
        send_list,
        kernel_weight.T,
        pixel_block.reshape(1, slots),
    )


def grid_kernel(
    core, below2, below1, here, above1, above2, sum_b2, sum_h, sum_a2, packed_own, packed_other, out,
    left, right, dense,
):
    me = core[0]
    for tile in range(CORES):
        pack = jnp.where(me == tile, packed_own[...], packed_other[...])
        weight = pack[0:KB, :]
        block = pack[KB : KB + 1, :]
        for number in range(PIX // KB):
            high, low = split(jnp.where(block == number, weight, 0.0))
            dense[tile, number * KB : (number + 1) * KB, :] = high
            dense[tile, PIX + number * KB : PIX + (number + 1) * KB, :] = low
    slabs = [
        (below2, sum_b2[0:1, :]),
        (below1.at[0], below2[TOTALS : TOTALS + 1, :]),
        (below1.at[1], below2[TOTALS + 1 : TOTALS + 2, :]),
        (here.at[0], sum_h[0:1, :]),
        (here.at[1], sum_h[1:2, :]),
        (above1.at[0], above2[0, TOTALS : TOTALS + 1, :]),
        (above1.at[1], above2[1, TOTALS : TOTALS + 1, :]),
        (above2.at[0], sum_a2[0:1, :]),
        (above2.at[1], sum_a2[1:2, :]),
    ]
    depth = REACH * SLAB
    totals = [jnp.zeros((1, PIX), f32) for _ in range(CORES)]
    sample = lax.broadcasted_iota(jnp.int32, (SLAB, SLAB), 0).astype(f32)
    lane = lax.broadcasted_iota(jnp.int32, (SLAB, SLAB), 1)
    for index, (unit, band_sum) in enumerate(slabs):
        scale = CH / band_sum
        high, low = split(unit[0:HALF_CH, :] * scale)
        at = index * SLAB
        left[:, at : at + SLAB] = high
        left[:, depth + at : depth + at + SLAB] = low
        left[:, 2 * depth + at : 2 * depth + at + SLAB] = high
        for tile in range(CORES):
            offset = tile + BAND - 1 - index
            columns = slice(tile * PIX, (tile + 1) * PIX)
            if not 0 <= offset < BAND:
                for copy in range(3):
                    start = copy * depth + at
                    right[start : start + SLAB, columns] = jnp.zeros((SLAB, PIX), bf16)
                continue
            pair = offset // 2
            chosen = unit[HALF_CH + pair : HALF_CH + pair + 1, :]
            hot = ((sample == chosen) & ((lane // CAP) == offset % 2)).astype(f32).astype(bf16)
            picked = lax.dot_general(
                hot,
                dense[tile, :, pair * SLAB : (pair + 1) * SLAB],
                (((1,), (1,)), ((), ())),
                preferred_element_type=f32,
            )
            top, rest = picked[:, 0:PIX], picked[:, PIX:]
            totals[tile] = totals[tile] + jnp.sum(top + rest, axis=0, keepdims=True)
            top, rest = top.astype(bf16), rest.astype(bf16)
            right[at : at + SLAB, columns] = top
            right[depth + at : depth + at + SLAB, columns] = top
            right[2 * depth + at : 2 * depth + at + SLAB, columns] = rest
    total = jnp.maximum(jnp.concatenate(totals, axis=1), 1.0)
    tiles = jnp.dot(left[...], right[...], preferred_element_type=f32) / total
    for row in range(CORES * TY):
        out[:, row] = tiles[:, row * TX : (row + 1) * TX].reshape(HALF_CH // 8, 8, TX)


def grid_tiles(core, units, sums, packed_own, packed_other):
    slots = BAND * CAP
    depth = REACH * SLAB
    return pl.pallas_call(
        grid_kernel,
        out_shape=jax.ShapeDtypeStruct((HALF_CH // 8, CORES * TY, 8, TX), f32),
        in_specs=[whole(pltpu.SMEM)] + [whole()] * 10,
        out_specs=whole(),
        scratch_shapes=[
            VMEM((HALF_CH, 3 * depth), bf16),
            VMEM((3 * depth, CORES * PIX), bf16),
            VMEM((CORES, 2 * PIX, slots), bf16),
        ],
        compiler_params=pltpu.CompilerParams(vmem_limit_bytes=32 << 20),
        name="grid_tiles",
    )(core, *units, *sums, packed_own, packed_other)


def waves(length):
    frequency = jnp.arange(length, dtype=jnp.int32)
    phases = (frequency[:, None] * frequency[None, :] % length).astype(f32) * (
        2.0 * math.pi / length
    )
    return jnp.concatenate([jnp.cos(phases), jnp.sin(phases)], axis=1)


def response(sigma, length):
    frequency = lax.broadcasted_iota(jnp.int32, (1, 2 * length), 1) % length
    folded = jnp.minimum(frequency, length - frequency).astype(f32) / length
    return jnp.exp(-2.0 * math.pi**2 * sigma**2 * folded**2)


def circulant(sigma, basis):
    length = basis.shape[0]
    return (
        lax.dot_general(
            basis * response(sigma, length),
            basis,
            (((1,), (1,)), ((), ())),
            precision=highest,
            preferred_element_type=f32,
        )
        / length
    )


def tables_kernel(sigma, row_waves, column_waves, rows_out, columns_out):
    width = sigma[pl.program_id(0)]
    high, low = split(circulant(width, row_waves[...]))
    rows_out[0, 0] = high
    rows_out[0, 1] = low
    high, low = split(circulant(width, column_waves[...]))
    columns_out[0, 0:TX, 0:TX] = high
    columns_out[0, 0:TX, TX:] = low
    columns_out[0, TX:, 0:TX] = high
    columns_out[0, TX:, TX:] = jnp.zeros_like(low)


def make_tables(sigma, length):
    channels = sigma.shape[0]
    waves_rows = waves(length)
    fixed = lambda shape: pl.BlockSpec(shape, lambda c: (0, 0))
    return pl.pallas_call(
        tables_kernel,
        grid=(channels,),
        out_shape=(
            jax.ShapeDtypeStruct((channels, 2, length, length), bf16),
            jax.ShapeDtypeStruct((channels, 2 * TX, 2 * TX), bf16),
        ),
        in_specs=[
            whole(pltpu.SMEM),
            fixed((length, 2 * length)),
            fixed((TX, 2 * TX)),
        ],
        out_specs=(
            pl.BlockSpec((1, 2, length, length), lambda c: (c, 0, 0, 0)),
            pl.BlockSpec((1, 2 * TX, 2 * TX), lambda c: (c, 0, 0)),
        ),
        compiler_params=pltpu.CompilerParams(vmem_limit_bytes=60 << 20),
        cost_estimate=pl.CostEstimate(
            flops=2 * channels * 6 * 2 * length**3, bytes_accessed=6 << 20, transcendentals=0
        ),
        name="smoothing_tables",
    )(sigma, waves_rows, waves(TX))


def smooth_kernel(
    field, rows_in, columns_in, out, rows_table, columns_table, across, smoothed, here, done
):
    channels, length, _ = smoothed.shape
    columns_copy = pltpu.make_async_copy(columns_in, columns_table, here.at[0])
    rows_copy = pltpu.make_async_copy(rows_in, rows_table, here.at[1])
    columns_copy.start()
    rows_copy.start()
    columns_copy.wait()
    for c in range(channels):
        high, low = split(field[pl.ds(c, length, stride=channels), :])
        both = jnp.dot(
            jnp.concatenate([high, low], axis=1), columns_table[c], preferred_element_type=f32
        )
        high, low = split(both[:, 0:TX] + both[:, TX:])
        across[c, :, 0:TX] = high
        across[c, :, TX:] = low
    rows_copy.wait()
    group = channels // GROUPS
    copies = []
    for number in range(GROUPS):
        for c in range(number * group, (number + 1) * group):
            both = jnp.dot(rows_table[c, 0], across[c], preferred_element_type=f32)
            rest = jnp.dot(rows_table[c, 1], across[c, :, 0:TX], preferred_element_type=f32)
            smoothed[c] = both[:, 0:TX] + both[:, TX:] + rest
        part = pl.ds(number * group, group)
        copies.append(pltpu.make_async_copy(smoothed.at[part], out.at[part], done.at[number]))
        copies[-1].start()
    for copy in copies:
        copy.wait()


def smooth(field, rows_table, columns_table):
    channels, _, length, _ = rows_table.shape
    return pl.pallas_call(
        smooth_kernel,
        out_shape=jax.ShapeDtypeStruct((channels, length, TX), f32),
        in_specs=[whole(), whole(pltpu.HBM), whole(pltpu.HBM)],
        out_specs=whole(pltpu.HBM),
        scratch_shapes=[
            VMEM(rows_table.shape, bf16),
            VMEM(columns_table.shape, bf16),
            VMEM((channels, length, 2 * TX), bf16),
            VMEM((channels, length, TX), f32),
            pltpu.SemaphoreType.DMA((2,)),
            pltpu.SemaphoreType.DMA((GROUPS,)),
        ],
        compiler_params=pltpu.CompilerParams(vmem_limit_bytes=VMEM_SMOOTH << 20),
        name="smooth",
    )(field, rows_table, columns_table)


def local(
    spectra, feed_ids, feed_gain, send_list, send_count, kernel_weight, pixel_block, beam_width
):
    chips = lax.axis_size(("y", "z"))

    def shift(array, by):
        return lax.ppermute(array, ("y", "z"), [(i, (i + by) % chips) for i in range(chips)])

    unit, packed = prepare(
        spectra, feed_ids, feed_gain, send_list, send_count, kernel_weight, pixel_block
    )
    here = lax.all_to_all(unit, "core", split_axis=0, concat_axis=0, tiled=True)
    packed_other = lax.ppermute(packed, "core", [(0, 1), (1, 0)])
    above1 = shift(here, -1)
    below1 = shift(here, 1)
    sums = lax.psum(here[:, TOTALS - 1, :], "chan")
    sum_a2, sum_b2 = shift(sums, -2), shift(sums[1:2], 2)
    above1 = above1.at[:, TOTALS, :].set(sums)
    above2 = shift(above1, -1)
    below2 = shift(below1[1].at[TOTALS : TOTALS + CORES, :].set(sums), 1)
    core = lax.axis_index("core").astype(jnp.int32).reshape(1)
    gridded = grid_tiles(
        core,
        (below2, below1, here, above1, above2),
        (sum_b2, sums, sum_a2),
        packed,
        packed_other,
    )
    gridded, beam_width = lax.optimization_barrier((gridded, beam_width))
    relaid = lax.all_to_all(gridded, ("y", "z"), split_axis=0, concat_axis=0, tiled=True)
    rows_table, columns_table = make_tables(beam_width, chips * CORES * TY)
    return smooth(relaid.reshape(chips * CORES * TY * 8, TX), rows_table, columns_table)


def solution(mesh):
    tiles, channels = mesh.devices.shape
    chips = tiles // CORES
    grid = Mesh(
        mesh.devices.reshape(chips // ROWS_Z, ROWS_Z, CORES, channels), ("y", "z", "core", "chan")
    )
    tile = ("y", "z", "core")
    in_specs = (
        P(tile, "chan"),
        P(tile),
        P(None, "chan"),
        P(tile, None),
        P(tile),
        P(tile, None),
        P(tile),
        P(("chan",) + tile),
    )
    out_specs = P(("chan",) + tile, None, None)
    return jax.shard_map(local, mesh=grid, in_specs=in_specs, out_specs=out_specs, check_vma=False)
```

```python
import math

import jax
import jax.numpy as jnp
from jax import lax
from jax.experimental import pallas as pl
from jax.experimental.pallas import tpu as pltpu
from jax.sharding import Mesh
from jax.sharding import PartitionSpec as P

CH = 4096
TY = 2
TX = 128
CORES = 2
ROWS_Z = 16
SLAB = 128
BAND = 8
CAP = 64
KB = 64
HALF_CH = 512
META = 8
UNIT = HALF_CH + META
SUM_ROW = HALF_CH + BAND // 2
REACH = 9
GROUPS = 4
VMEM_SMOOTH = 52
VMEM_PREPARE = 56
PIX = TY * TX

f32 = jnp.float32
bf16 = jnp.bfloat16
highest = lax.Precision.HIGHEST
VMEM = pltpu.VMEM


def whole(memory_space=VMEM):
    return pl.BlockSpec(memory_space=memory_space)


def split(value):
    high = value.astype(bf16)
    return high, (value - high.astype(f32)).astype(bf16)


def prepare_kernel(
    counts,
    spectra_in,
    feed_ids_in,
    feed_gain_in,
    send_list_in,
    weights_in,
    blocks_in,
    unit,
    packed,
    spectra,
    feed_ids,
    feed_gain,
    gains,
    send_list,
    blocks,
    arrived,
):
    feeds = feed_gain_in.shape[0]
    copies = []
    for source, target in (
        (feed_ids_in, feed_ids),
        (feed_gain_in, feed_gain),
        (spectra_in, spectra),
        (send_list_in, send_list),
        (blocks_in, blocks),
        (weights_in, packed.at[0:KB]),
    ):
        copies.append(pltpu.make_async_copy(source, target, arrived.at[len(copies)]))
        copies[-1].start()
    gains[...] = jnp.zeros_like(gains)
    copies[0].wait()
    copies[1].wait()
    gains[0:feeds, :] = feed_gain[...]
    onehot = (lax.broadcasted_iota(jnp.int32, (gains.shape[0], SLAB), 0) == feed_ids[...]).astype(
        f32
    )
    gain_rows = lax.dot_general(
        gains[...], onehot, (((0,), (0,)), ((), ())), precision=highest, preferred_element_type=f32
    )
    copies[2].wait()
    raw = spectra[...].T
    band_sum = jnp.sum(raw, axis=0, keepdims=True)
    scaled = (raw * gain_rows).reshape(HALF_CH // 8, CORES, 8, SLAB)
    copies[3].wait()
    lane = lax.broadcasted_iota(jnp.int32, (1, CAP), 1)
    rows = [
        jnp.where(lane < counts[row], send_list[row : row + 1, :], -1).astype(f32)
        for row in range(BAND)
    ]
    rows = [jnp.concatenate(rows[2 * m : 2 * m + 2], axis=1) for m in range(BAND // 2)]
    meta = jnp.concatenate(rows + [band_sum, jnp.zeros((META - BAND // 2 - 1, SLAB), f32)], axis=0)
    for core in range(CORES):
        unit[core, 0:HALF_CH, :] = scaled[:, core].reshape(HALF_CH, SLAB)
        unit[core, HALF_CH:UNIT, :] = meta
    copies[4].wait()
    packed[KB : KB + 8, :] = jnp.broadcast_to(blocks[...].astype(f32), (8, BAND * CAP))
    copies[5].wait()


def prepare(spectra, feed_ids, feed_gain, send_list, send_count, kernel_weight, pixel_block):
    slots = BAND * CAP
    channels = spectra.shape[1]
    return pl.pallas_call(
        prepare_kernel,
        out_shape=(
            jax.ShapeDtypeStruct((CORES, UNIT, SLAB), f32),
            jax.ShapeDtypeStruct((KB + 8, slots), f32),
        ),
        in_specs=[whole(pltpu.SMEM)] + [whole(pltpu.HBM)] * 6,
        out_specs=(whole(), whole()),
        scratch_shapes=[
            VMEM((SLAB, channels), f32),
            VMEM((1, SLAB), jnp.int32),
            VMEM(feed_gain.shape, f32),
            VMEM((24, channels), f32),
            VMEM((BAND, CAP), jnp.int32),
            VMEM((1, slots), jnp.int32),
            pltpu.SemaphoreType.DMA((6,)),
        ],
        compiler_params=pltpu.CompilerParams(vmem_limit_bytes=VMEM_PREPARE << 20),
        name="prepare",
    )(
        send_count,
        spectra,
        feed_ids.reshape(1, SLAB),
        feed_gain,
        send_list,
        kernel_weight.T,
        pixel_block.reshape(1, slots),
    )


def grid_kernel(
    below2, below1, here, above1, above2, sums, packed_even, packed_odd, out, left, right, dense
):
    for tile, pack in enumerate((packed_even, packed_odd)):
        weight = pack[0:KB, :]
        block = pack[KB : KB + 1, :]
        for number in range(PIX // KB):
            high, low = split(jnp.where(block == number, weight, 0.0))
            dense[tile, number * KB : (number + 1) * KB, :] = high
            dense[tile, PIX + number * KB : PIX + (number + 1) * KB, :] = low
    slabs = [
        below2,
        below1.at[0],
        below1.at[1],
        here.at[0],
        here.at[1],
        above1.at[0],
        above1.at[1],
        above2.at[0],
        above2.at[1],
    ]
    depth = REACH * SLAB
    totals = [jnp.zeros((1, PIX), f32) for _ in range(CORES)]
    sample = lax.broadcasted_iota(jnp.int32, (SLAB, SLAB), 0).astype(f32)
    lane = lax.broadcasted_iota(jnp.int32, (SLAB, SLAB), 1)
    for index, unit in enumerate(slabs):
        scale = CH / sums[index : index + 1, :]
        high, low = split(unit[0:HALF_CH, :] * scale)
        at = index * SLAB
        left[:, at : at + SLAB] = high
        left[:, depth + at : depth + at + SLAB] = low
        left[:, 2 * depth + at : 2 * depth + at + SLAB] = high
        for tile in range(CORES):
            offset = tile + BAND - 1 - index
            columns = slice(tile * PIX, (tile + 1) * PIX)
            if not 0 <= offset < BAND:
                for copy in range(3):
                    start = copy * depth + at
                    right[start : start + SLAB, columns] = jnp.zeros((SLAB, PIX), bf16)
                continue
            pair = offset // 2
            chosen = unit[HALF_CH + pair : HALF_CH + pair + 1, :]
            hot = ((sample == chosen) & ((lane // CAP) == offset % 2)).astype(f32).astype(bf16)
            picked = lax.dot_general(
                hot,
                dense[tile, :, pair * SLAB : (pair + 1) * SLAB],
                (((1,), (1,)), ((), ())),
                preferred_element_type=f32,
            )
            top, rest = picked[:, 0:PIX], picked[:, PIX:]
            totals[tile] = totals[tile] + jnp.sum(top + rest, axis=0, keepdims=True)
            top, rest = top.astype(bf16), rest.astype(bf16)
            right[at : at + SLAB, columns] = top
            right[depth + at : depth + at + SLAB, columns] = top
            right[2 * depth + at : 2 * depth + at + SLAB, columns] = rest
    total = jnp.maximum(jnp.concatenate(totals, axis=1), 1.0)
    tiles = jnp.dot(left[...], right[...], preferred_element_type=f32) / total
    for row in range(CORES * TY):
        out[:, row] = tiles[:, row * TX : (row + 1) * TX].reshape(HALF_CH // 8, 8, TX)


def grid_tiles(units, sums, packed_even, packed_odd):
    slots = BAND * CAP
    depth = REACH * SLAB
    return pl.pallas_call(
        grid_kernel,
        out_shape=jax.ShapeDtypeStruct((HALF_CH // 8, CORES * TY, 8, TX), f32),
        in_specs=[whole()] * 8,
        out_specs=whole(),
        scratch_shapes=[
            VMEM((HALF_CH, 3 * depth), bf16),
            VMEM((3 * depth, CORES * PIX), bf16),
            VMEM((CORES, 2 * PIX, slots), bf16),
        ],
        compiler_params=pltpu.CompilerParams(vmem_limit_bytes=32 << 20),
        name="grid_tiles",
    )(*units, sums, packed_even, packed_odd)


def waves(length):
    frequency = jnp.arange(length, dtype=jnp.int32)
    phases = (frequency[:, None] * frequency[None, :] % length).astype(f32) * (
        2.0 * math.pi / length
    )
    return jnp.concatenate([jnp.cos(phases), jnp.sin(phases)], axis=1)


def response(sigma, length):
    frequency = lax.broadcasted_iota(jnp.int32, (1, 2 * length), 1) % length
    folded = jnp.minimum(frequency, length - frequency).astype(f32) / length
    return jnp.exp(-2.0 * math.pi**2 * sigma**2 * folded**2)


def circulant(sigma, basis):
    length = basis.shape[0]
    return (
        lax.dot_general(
            basis * response(sigma, length),
            basis,
            (((1,), (1,)), ((), ())),
            precision=highest,
            preferred_element_type=f32,
        )
        / length
    )


def tables_kernel(sigma, row_waves, column_waves, rows_out, columns_out):
    width = sigma[pl.program_id(0)]
    high, low = split(circulant(width, row_waves[...]))
    rows_out[0, 0] = high
    rows_out[0, 1] = low
    high, low = split(circulant(width, column_waves[...]))
    columns_out[0, 0:TX, 0:TX] = high
    columns_out[0, 0:TX, TX:] = low
    columns_out[0, TX:, 0:TX] = high
    columns_out[0, TX:, TX:] = jnp.zeros_like(low)


def make_tables(sigma, length):
    channels = sigma.shape[0]
    waves_rows = waves(length)
    fixed = lambda shape: pl.BlockSpec(shape, lambda c: (0, 0))
    return pl.pallas_call(
        tables_kernel,
        grid=(channels,),
        out_shape=(
            jax.ShapeDtypeStruct((channels, 2, length, length), bf16),
            jax.ShapeDtypeStruct((channels, 2 * TX, 2 * TX), bf16),
        ),
        in_specs=[
            whole(pltpu.SMEM),
            fixed((length, 2 * length)),
            fixed((TX, 2 * TX)),
        ],
        out_specs=(
            pl.BlockSpec((1, 2, length, length), lambda c: (c, 0, 0, 0)),
            pl.BlockSpec((1, 2 * TX, 2 * TX), lambda c: (c, 0, 0)),
        ),
        compiler_params=pltpu.CompilerParams(vmem_limit_bytes=60 << 20),
        cost_estimate=pl.CostEstimate(
            flops=2 * channels * 6 * 2 * length**3, bytes_accessed=6 << 20, transcendentals=0
        ),
        name="smoothing_tables",
    )(sigma, waves_rows, waves(TX))


def smooth_kernel(
    field, rows_in, columns_in, out, rows_table, columns_table, across, smoothed, here, done
):
    channels, length, _ = smoothed.shape
    columns_copy = pltpu.make_async_copy(columns_in, columns_table, here.at[0])
    rows_copy = pltpu.make_async_copy(rows_in, rows_table, here.at[1])
    columns_copy.start()
    rows_copy.start()
    columns_copy.wait()
    for c in range(channels):
        high, low = split(field[pl.ds(c, length, stride=channels), :])
        both = jnp.dot(
            jnp.concatenate([high, low], axis=1), columns_table[c], preferred_element_type=f32
        )
        high, low = split(both[:, 0:TX] + both[:, TX:])
        across[c, :, 0:TX] = high
        across[c, :, TX:] = low
    rows_copy.wait()
    group = channels // GROUPS
    copies = []
    for number in range(GROUPS):
        for c in range(number * group, (number + 1) * group):
            both = jnp.dot(rows_table[c, 0], across[c], preferred_element_type=f32)
            rest = jnp.dot(rows_table[c, 1], across[c, :, 0:TX], preferred_element_type=f32)
            smoothed[c] = both[:, 0:TX] + both[:, TX:] + rest
        part = pl.ds(number * group, group)
        copies.append(pltpu.make_async_copy(smoothed.at[part], out.at[part], done.at[number]))
        copies[-1].start()
    for copy in copies:
        copy.wait()


def smooth(field, rows_table, columns_table):
    channels, _, length, _ = rows_table.shape
    return pl.pallas_call(
        smooth_kernel,
        out_shape=jax.ShapeDtypeStruct((channels, length, TX), f32),
        in_specs=[whole(), whole(pltpu.HBM), whole(pltpu.HBM)],
        out_specs=whole(pltpu.HBM),
        scratch_shapes=[
            VMEM(rows_table.shape, bf16),
            VMEM(columns_table.shape, bf16),
            VMEM((channels, length, 2 * TX), bf16),
            VMEM((channels, length, TX), f32),
            pltpu.SemaphoreType.DMA((2,)),
            pltpu.SemaphoreType.DMA((GROUPS,)),
        ],
        compiler_params=pltpu.CompilerParams(vmem_limit_bytes=VMEM_SMOOTH << 20),
        name="smooth",
    )(field, rows_table, columns_table)


def local(
    spectra, feed_ids, feed_gain, send_list, send_count, kernel_weight, pixel_block, beam_width
):
    chips = lax.axis_size(("y", "z"))

    def shift(array, by):
        return lax.ppermute(array, ("y", "z"), [(i, (i + by) % chips) for i in range(chips)])

    unit, packed = prepare(
        spectra, feed_ids, feed_gain, send_list, send_count, kernel_weight, pixel_block
    )
    here = lax.all_to_all(unit, "core", split_axis=0, concat_axis=0, tiled=True)
    packed_other = lax.ppermute(packed, "core", [(0, 1), (1, 0)])
    part = here[:, SUM_ROW, :]
    arrived = (
        shift(here, -1),
        shift(here, 1),
        shift(part, -2),
        shift(part[1:2], 2),
        packed_other,
    )
    above1, below1, part_above2, part_below2, packed_other = lax.optimization_barrier(arrived)
    above2 = shift(above1, -1)
    below2 = shift(below1[1], 1)
    parts = [part_below2, below1[:, SUM_ROW, :], part, above1[:, SUM_ROW, :], part_above2]
    sums = lax.psum(jnp.concatenate(parts, axis=0), "chan")
    even = lax.axis_index("core") == 0
    gridded = grid_tiles(
        (below2, below1, here, above1, above2),
        sums,
        jnp.where(even, packed, packed_other),
        jnp.where(even, packed_other, packed),
    )
    gridded, beam_width = lax.optimization_barrier((gridded, beam_width))
    relaid = lax.all_to_all(gridded, ("y", "z"), split_axis=0, concat_axis=0, tiled=True)
    rows_table, columns_table = make_tables(beam_width, chips * CORES * TY)
    return smooth(relaid.reshape(chips * CORES * TY * 8, TX), rows_table, columns_table)


def solution(mesh):
    tiles, channels = mesh.devices.shape
    chips = tiles // CORES
    grid = Mesh(
        mesh.devices.reshape(chips // ROWS_Z, ROWS_Z, CORES, channels), ("y", "z", "core", "chan")
    )
    tile = ("y", "z", "core")
    in_specs = (
        P(tile, "chan"),
        P(tile),
        P(None, "chan"),
        P(tile, None),
        P(tile),
        P(tile, None),
        P(tile),
        P(("chan",) + tile),
    )
    out_specs = P(("chan",) + tile, None, None)
    return jax.shard_map(local, mesh=grid, in_specs=in_specs, out_specs=out_specs, check_vma=False)
```

```python
import math

import jax
import jax.numpy as jnp
from jax import lax
from jax.experimental import pallas as pl
from jax.experimental.pallas import tpu as pltpu
from jax.sharding import Mesh
from jax.sharding import PartitionSpec as P

CH = 4096
TY = 2
TX = 128
CORES = 2
ROWS_Z = 16
SLAB = 128
BAND = 8
CAP = 64
KB = 64
HALF_CH = 512
META = 8
UNIT = HALF_CH + META
REACH = 9
GROUPS = 8
PARTS = 4
VMEM_SMOOTH = 52
VMEM_PREPARE = 56
PIX = TY * TX

f32 = jnp.float32
bf16 = jnp.bfloat16
highest = lax.Precision.HIGHEST
VMEM = pltpu.VMEM


def whole(memory_space=VMEM):
    return pl.BlockSpec(memory_space=memory_space)


def split(value):
    high = value.astype(bf16)
    return high, (value - high.astype(f32)).astype(bf16)


def prepare_kernel(
    counts_in,
    spectra_in,
    feed_ids_in,
    feed_gain_in,
    send_list_in,
    weights_in,
    blocks_in,
    unit_out,
    packed_out,
    counts,
    spectra,
    feed_ids,
    feed_gain,
    gains,
    send_list,
    blocks,
    unit,
    packed,
    arrived,
    left,
):
    feeds, channels = feed_gain.shape
    width = channels // PARTS
    rows = HALF_CH // PARTS
    room = gains.shape[0] // 3
    copies = []

    def fetch(source, target):
        copies.append(pltpu.make_async_copy(source, target, arrived.at[len(copies)]))
        copies[-1].start()

    fetch(feed_ids_in, feed_ids)
    fetch(feed_gain_in, feed_gain)
    for part in range(PARTS):
        columns = pl.ds(part * width, width)
        fetch(spectra_in.at[:, columns], spectra.at[part])
    fetch(send_list_in, send_list)
    fetch(blocks_in, blocks)
    fetch(weights_in, packed.at[0:KB])
    fetch(counts_in, counts)
    gains[...] = jnp.zeros_like(gains)
    copies[0].wait()
    copies[1].wait()
    value = feed_gain[...]
    for step in range(3):
        piece = value.astype(bf16)
        value = value - piece.astype(f32)
        gains[step * room : step * room + feeds, :] = piece.astype(f32)
    onehot = (
        lax.broadcasted_iota(jnp.int32, (3 * room, SLAB), 0) % room == feed_ids[...]
    ).astype(f32)
    onehot = onehot.astype(bf16)
    band_sum = jnp.zeros((1, SLAB), f32)
    sends = []

    def send(source, target):
        sends.append(pltpu.make_async_copy(source, target, left.at[len(sends)]))
        sends[-1].start()

    for part in range(PARTS):
        gain_rows = lax.dot_general(
            gains[:, part * width : (part + 1) * width].astype(bf16),
            onehot,
            (((0,), (0,)), ((), ())),
            preferred_element_type=f32,
        )
        copies[2 + part].wait()
        raw = spectra[part].T
        band_sum = band_sum + jnp.sum(raw, axis=0, keepdims=True)
        scaled = (raw * gain_rows).reshape(rows // 8, CORES, 8, SLAB)
        for core in range(CORES):
            unit[core, part * rows : (part + 1) * rows, :] = scaled[:, core].reshape(rows, SLAB)
        span = pl.ds(part * rows, rows)
        send(unit.at[:, span], unit_out.at[:, span])
    copies[2 + PARTS].wait()
    copies[5 + PARTS].wait()
    lane = lax.broadcasted_iota(jnp.int32, (1, CAP), 1)
    lists = [
        jnp.where(lane < counts[row], send_list[row : row + 1, :], -1).astype(f32)
        for row in range(BAND)
    ]
    lists = [jnp.concatenate(lists[2 * m : 2 * m + 2], axis=1) for m in range(BAND // 2)]
    meta = jnp.concatenate(lists + [band_sum, jnp.zeros((META - BAND // 2 - 1, SLAB), f32)], axis=0)
    for core in range(CORES):
        unit[core, HALF_CH:UNIT, :] = meta
    span = pl.ds(HALF_CH, META)
    send(unit.at[:, span], unit_out.at[:, span])
    copies[3 + PARTS].wait()
    packed[KB : KB + 8, :] = jnp.broadcast_to(blocks[...].astype(f32), (8, BAND * CAP))
    copies[4 + PARTS].wait()
    send(packed, packed_out)
    for copy in sends:
        copy.wait()


def prepare(spectra, feed_ids, feed_gain, send_list, send_count, kernel_weight, pixel_block):
    slots = BAND * CAP
    channels = spectra.shape[1]
    unit = (CORES, UNIT, SLAB)
    packed = (KB + 8, slots)
    return pl.pallas_call(
        prepare_kernel,
        out_shape=(jax.ShapeDtypeStruct(unit, f32), jax.ShapeDtypeStruct(packed, f32)),
        in_specs=[whole(pltpu.HBM)] * 7,
        out_specs=(whole(pltpu.HBM), whole(pltpu.HBM)),
        scratch_shapes=[
            pltpu.SMEM(send_count.shape, jnp.int32),
            VMEM((PARTS, SLAB, channels // PARTS), f32),
            VMEM((1, SLAB), jnp.int32),
            VMEM(feed_gain.shape, f32),
            VMEM((3 * 32, channels), f32),
            VMEM((BAND, CAP), jnp.int32),
            VMEM((1, slots), jnp.int32),
            VMEM(unit, f32),
            VMEM(packed, f32),
            pltpu.SemaphoreType.DMA((6 + PARTS,)),
            pltpu.SemaphoreType.DMA((2 + PARTS,)),
        ],
        compiler_params=pltpu.CompilerParams(vmem_limit_bytes=VMEM_PREPARE << 20),
        name="prepare",
    )(
        send_count,
        spectra,
        feed_ids.reshape(1, SLAB),
        feed_gain,
        send_list,
        kernel_weight.T,
        pixel_block.reshape(1, slots),
    )


def grid_kernel(
    below2, below1, here, above1, above2, sums, packed_even, packed_odd, out,
    left_high, left_low, right, dense, tiles, done,
):
    for tile, pack in enumerate((packed_even, packed_odd)):
        weight = pack[0:KB, :]
        block = pack[KB : KB + 1, :]
        for number in range(PIX // KB):
            high, low = split(jnp.where(block == number, weight, 0.0))
            dense[tile, number * KB : (number + 1) * KB, :] = high
            dense[tile, PIX + number * KB : PIX + (number + 1) * KB, :] = low
    first, second = pl.ds(0, UNIT), pl.ds(UNIT, UNIT)
    slabs = [
        here.at[first],
        here.at[second],
        below1.at[first],
        below1.at[second],
        above1.at[first],
        above1.at[second],
        below2,
        above2.at[first],
        above2.at[second],
    ]
    places = [3, 4, 1, 2, 5, 6, 0, 7, 8]
    totals = [jnp.zeros((1, PIX), f32) for _ in range(CORES)]
    sample = lax.broadcasted_iota(jnp.int32, (SLAB, SLAB), 0).astype(f32)
    lane = lax.broadcasted_iota(jnp.int32, (SLAB, SLAB), 1)
    for index, unit in zip(places, slabs):
        scale = CH / sums[index : index + 1, :]
        high, low = split(unit[0:HALF_CH, :] * scale)
        at = index * SLAB
        left_high[:, at : at + SLAB] = high
        left_low[:, at : at + SLAB] = low
        for tile in range(CORES):
            offset = tile + BAND - 1 - index
            if not 0 <= offset < BAND:
                continue
            pair = offset // 2
            chosen = unit[HALF_CH + pair : HALF_CH + pair + 1, :]
            hot = ((sample == chosen) & ((lane // CAP) == offset % 2)).astype(f32).astype(bf16)
            picked = lax.dot_general(
                hot,
                dense[tile, :, pair * SLAB : (pair + 1) * SLAB],
                (((1,), (1,)), ((), ())),
                preferred_element_type=f32,
            )
            totals[tile] = totals[tile] + jnp.sum(
                picked[:, 0:PIX] + picked[:, PIX:], axis=0, keepdims=True
            )
            start = (index - tile) * SLAB
            right[tile, start : start + SLAB, :] = picked.astype(bf16)
    copies = []
    for tile in range(CORES):
        span = slice(tile * SLAB, (tile + BAND) * SLAB)
        both = jnp.dot(left_high[:, span], right[tile], preferred_element_type=f32)
        rest = jnp.dot(left_low[:, span], right[tile, :, 0:PIX], preferred_element_type=f32)
        gridded = (both[:, 0:PIX] + both[:, PIX:] + rest) / jnp.maximum(totals[tile], 1.0)
        for row in range(TY):
            out[:, tile * TY + row] = gridded[:, row * TX : (row + 1) * TX].reshape(
                HALF_CH // 8, 8, TX
            )


def grid_tiles(units, sums, packed_even, packed_odd):
    slots = BAND * CAP
    depth = REACH * SLAB
    return pl.pallas_call(
        grid_kernel,
        out_shape=jax.ShapeDtypeStruct((HALF_CH // 8, CORES * TY, 8, TX), f32),
        in_specs=[whole()] * 8,
        out_specs=whole(),
        scratch_shapes=[
            VMEM((HALF_CH, depth), bf16),
            VMEM((HALF_CH, depth), bf16),
            VMEM((CORES, BAND * SLAB, 2 * PIX), bf16),
            VMEM((CORES, 2 * PIX, slots), bf16),
            VMEM((CORES, HALF_CH // 8, TY, 8, TX), f32),
            pltpu.SemaphoreType.DMA((CORES,)),
        ],
        compiler_params=pltpu.CompilerParams(vmem_limit_bytes=32 << 20),
        name="grid_tiles",
    )(*units, sums, packed_even, packed_odd)


def waves(length):
    frequency = jnp.arange(length, dtype=jnp.int32)
    phases = (frequency[:, None] * frequency[None, :] % length).astype(f32) * (
        2.0 * math.pi / length
    )
    return jnp.concatenate([jnp.cos(phases), jnp.sin(phases)], axis=1)


def response(sigma, length):
    frequency = lax.broadcasted_iota(jnp.int32, (1, 2 * length), 1) % length
    folded = jnp.minimum(frequency, length - frequency).astype(f32) / length
    return jnp.exp(-2.0 * math.pi**2 * sigma**2 * folded**2)


def circulant(sigma, basis):
    length = basis.shape[0]
    return (
        lax.dot_general(
            basis * response(sigma, length),
            basis,
            (((1,), (1,)), ((), ())),
            precision=highest,
            preferred_element_type=f32,
        )
        / length
    )


def tables_kernel(sigma, row_waves, column_waves, rows_out, columns_out):
    width = sigma[pl.program_id(0)]
    high, low = split(circulant(width, row_waves[...]))
    rows_out[0, 0] = high
    rows_out[0, 1] = low
    high, low = split(circulant(width, column_waves[...]))
    columns_out[0, 0:TX, 0:TX] = high
    columns_out[0, 0:TX, TX:] = low
    columns_out[0, TX:, 0:TX] = high
    columns_out[0, TX:, TX:] = jnp.zeros_like(low)


def make_tables(sigma, length):
    channels = sigma.shape[0]
    waves_rows = waves(length)
    fixed = lambda shape: pl.BlockSpec(shape, lambda c: (0, 0))
    return pl.pallas_call(
        tables_kernel,
        grid=(channels,),
        out_shape=(
            jax.ShapeDtypeStruct((channels, 2, length, length), bf16),
            jax.ShapeDtypeStruct((channels, 2 * TX, 2 * TX), bf16),
        ),
        in_specs=[
            whole(pltpu.SMEM),
            fixed((length, 2 * length)),
            fixed((TX, 2 * TX)),
        ],
        out_specs=(
            pl.BlockSpec((1, 2, length, length), lambda c: (c, 0, 0, 0)),
            pl.BlockSpec((1, 2 * TX, 2 * TX), lambda c: (c, 0, 0)),
        ),
        compiler_params=pltpu.CompilerParams(vmem_limit_bytes=60 << 20),
        cost_estimate=pl.CostEstimate(
            flops=2 * channels * 6 * 2 * length**3, bytes_accessed=6 << 20, transcendentals=0
        ),
        name="smoothing_tables",
    )(sigma, waves_rows, waves(TX))


def smooth_kernel(
    field, rows_in, columns_in, out, rows_table, columns_table, across, smoothed, here, done
):
    channels, length, _ = smoothed.shape
    columns_copy = pltpu.make_async_copy(columns_in, columns_table, here.at[0])
    rows_copy = pltpu.make_async_copy(rows_in, rows_table, here.at[1])
    columns_copy.start()
    rows_copy.start()
    columns_copy.wait()
    for c in range(channels):
        high, low = split(field[pl.ds(c, length, stride=channels), :])
        both = jnp.dot(
            jnp.concatenate([high, low], axis=1), columns_table[c], preferred_element_type=f32
        )
        high, low = split(both[:, 0:TX] + both[:, TX:])
        across[c, :, 0:TX] = high
        across[c, :, TX:] = low
    rows_copy.wait()
    group = channels // GROUPS
    copies = []
    for number in range(GROUPS):
        for c in range(number * group, (number + 1) * group):
            both = jnp.dot(rows_table[c, 0], across[c], preferred_element_type=f32)
            rest = jnp.dot(rows_table[c, 1], across[c, :, 0:TX], preferred_element_type=f32)
            smoothed[c] = both[:, 0:TX] + both[:, TX:] + rest
        part = pl.ds(number * group, group)
        copies.append(pltpu.make_async_copy(smoothed.at[part], out.at[part], done.at[number]))
        copies[-1].start()
    for copy in copies:
        copy.wait()


def smooth(field, rows_table, columns_table):
    channels, _, length, _ = rows_table.shape
    return pl.pallas_call(
        smooth_kernel,
        out_shape=jax.ShapeDtypeStruct((channels, length, TX), f32),
        in_specs=[whole(), whole(pltpu.HBM), whole(pltpu.HBM)],
        out_specs=whole(pltpu.HBM),
        scratch_shapes=[
            VMEM(rows_table.shape, bf16),
            VMEM(columns_table.shape, bf16),
            VMEM((channels, length, 2 * TX), bf16),
            VMEM((channels, length, TX), f32),
            pltpu.SemaphoreType.DMA((2,)),
            pltpu.SemaphoreType.DMA((GROUPS,)),
        ],
        compiler_params=pltpu.CompilerParams(vmem_limit_bytes=VMEM_SMOOTH << 20),
        name="smooth",
    )(field, rows_table, columns_table)


def sum_rows(block):
    starts = range(HALF_CH + BAND // 2, block.shape[0], UNIT)
    return jnp.concatenate([block[start : start + 1] for start in starts], axis=0)


def local(
    spectra, feed_ids, feed_gain, send_list, send_count, kernel_weight, pixel_block, beam_width
):
    chips = lax.axis_size(("y", "z"))

    def shift(array, by):
        return lax.ppermute(array, ("y", "z"), [(i, (i + by) % chips) for i in range(chips)])

    unit, packed = prepare(
        spectra, feed_ids, feed_gain, send_list, send_count, kernel_weight, pixel_block
    )
    unit = unit.reshape(CORES * UNIT, SLAB)
    here = lax.all_to_all(unit, "core", split_axis=0, concat_axis=0, tiled=True)
    packed_other = lax.ppermute(packed, "core", [(0, 1), (1, 0)])
    above1, below1 = shift(here, -1), shift(here, 1)
    part_above2 = shift(sum_rows(here), -2)
    part_below2 = shift(sum_rows(here)[1:], 2)
    above2 = shift(above1, -1)
    below2 = shift(below1[UNIT:], 1)
    parts = [part_below2] + [sum_rows(block) for block in (below1, here, above1)] + [part_above2]
    sums = lax.psum(jnp.concatenate(parts, axis=0), "chan")
    even = lax.axis_index("core") == 0
    gridded = grid_tiles(
        (below2, below1, here, above1, above2),
        sums,
        jnp.where(even, packed, packed_other),
        jnp.where(even, packed_other, packed),
    )
    gridded, beam_width = lax.optimization_barrier((gridded, beam_width))
    relaid = lax.all_to_all(gridded, ("y", "z"), split_axis=0, concat_axis=0, tiled=True)
    rows_table, columns_table = make_tables(beam_width, chips * CORES * TY)
    return smooth(relaid.reshape(chips * CORES * TY * 8, TX), rows_table, columns_table)


def solution(mesh):
    tiles, channels = mesh.devices.shape
    chips = tiles // CORES
    grid = Mesh(
        mesh.devices.reshape(chips // ROWS_Z, ROWS_Z, CORES, channels), ("y", "z", "core", "chan")
    )
    tile = ("y", "z", "core")
    in_specs = (
        P(tile, "chan"),
        P(tile),
        P(None, "chan"),
        P(tile, None),
        P(tile),
        P(tile, None),
        P(tile),
        P(("chan",) + tile),
    )
    out_specs = P(("chan",) + tile, None, None)
    return jax.shard_map(local, mesh=grid, in_specs=in_specs, out_specs=out_specs, check_vma=False)
```

```python
import math

import jax
import jax.numpy as jnp
from jax import lax
from jax.experimental import pallas as pl
from jax.experimental.pallas import tpu as pltpu
from jax.sharding import Mesh
from jax.sharding import PartitionSpec as P

CH = 4096
TY = 2
TX = 128
CORES = 2
ROWS_Z = 16
SLAB = 128
BAND = 8
CAP = 64
KB = 64
HALF_CH = 512
META = 8
UNIT = HALF_CH + META
REACH = 9
GROUPS = 8
PARTS = 4
VMEM_SMOOTH = 52
VMEM_PREPARE = 56
PIX = TY * TX

f32 = jnp.float32
bf16 = jnp.bfloat16
highest = lax.Precision.HIGHEST
VMEM = pltpu.VMEM


def whole(memory_space=VMEM):
    return pl.BlockSpec(memory_space=memory_space)


def split(value):
    high = value.astype(bf16)
    return high, (value - high.astype(f32)).astype(bf16)


def prepare_kernel(
    counts_in,
    spectra_in,
    feed_ids_in,
    feed_gain_in,
    send_list_in,
    weights_in,
    blocks_in,
    unit_out,
    packed_out,
    counts,
    spectra,
    feed_ids,
    feed_gain,
    gains,
    send_list,
    blocks,
    unit,
    packed,
    arrived,
    left,
):
    feeds, channels = feed_gain.shape
    width = channels // PARTS
    rows = HALF_CH // PARTS
    room = gains.shape[0] // 3
    copies = []

    def fetch(source, target):
        copies.append(pltpu.make_async_copy(source, target, arrived.at[len(copies)]))
        copies[-1].start()

    fetch(feed_ids_in, feed_ids)
    fetch(feed_gain_in, feed_gain)
    for part in range(PARTS):
        columns = pl.ds(part * width, width)
        fetch(spectra_in.at[:, columns], spectra.at[part])
    fetch(send_list_in, send_list)
    fetch(blocks_in, blocks)
    fetch(weights_in, packed.at[0:KB])
    fetch(counts_in, counts)
    gains[...] = jnp.zeros_like(gains)
    copies[0].wait()
    copies[1].wait()
    value = feed_gain[...]
    for step in range(3):
        piece = value.astype(bf16)
        value = value - piece.astype(f32)
        gains[step * room : step * room + feeds, :] = piece.astype(f32)
    onehot = (
        lax.broadcasted_iota(jnp.int32, (3 * room, SLAB), 0) % room == feed_ids[...]
    ).astype(f32)
    onehot = onehot.astype(bf16)
    band_sum = jnp.zeros((1, SLAB), f32)
    sends = []

    def send(source, target):
        sends.append(pltpu.make_async_copy(source, target, left.at[len(sends)]))
        sends[-1].start()

    for part in range(PARTS):
        gain_rows = lax.dot_general(
            gains[:, part * width : (part + 1) * width].astype(bf16),
            onehot,
            (((0,), (0,)), ((), ())),
            preferred_element_type=f32,
        )
        copies[2 + part].wait()
        raw = spectra[part].T
        band_sum = band_sum + jnp.sum(raw, axis=0, keepdims=True)
        scaled = (raw * gain_rows).reshape(rows // 8, CORES, 8, SLAB)
        for core in range(CORES):
            unit[core, part * rows : (part + 1) * rows, :] = scaled[:, core].reshape(rows, SLAB)
        span = pl.ds(part * rows, rows)
        send(unit.at[:, span], unit_out.at[:, span])
    copies[2 + PARTS].wait()
    copies[5 + PARTS].wait()
    lane = lax.broadcasted_iota(jnp.int32, (1, CAP), 1)
    lists = [
        jnp.where(lane < counts[row], send_list[row : row + 1, :], -1).astype(f32)
        for row in range(BAND)
    ]
    lists = [jnp.concatenate(lists[2 * m : 2 * m + 2], axis=1) for m in range(BAND // 2)]
    meta = jnp.concatenate(lists + [band_sum, jnp.zeros((META - BAND // 2 - 1, SLAB), f32)], axis=0)
    for core in range(CORES):
        unit[core, HALF_CH:UNIT, :] = meta
    span = pl.ds(HALF_CH, META)
    send(unit.at[:, span], unit_out.at[:, span])
    copies[3 + PARTS].wait()
    packed[KB : KB + 8, :] = jnp.broadcast_to(blocks[...].astype(f32), (8, BAND * CAP))
    copies[4 + PARTS].wait()
    send(packed, packed_out)
    for copy in sends:
        copy.wait()


def prepare(spectra, feed_ids, feed_gain, send_list, send_count, kernel_weight, pixel_block):
    slots = BAND * CAP
    channels = spectra.shape[1]
    unit = (CORES, UNIT, SLAB)
    packed = (KB + 8, slots)
    return pl.pallas_call(
        prepare_kernel,
        out_shape=(jax.ShapeDtypeStruct(unit, f32), jax.ShapeDtypeStruct(packed, f32)),
        in_specs=[whole(pltpu.HBM)] * 7,
        out_specs=(whole(pltpu.HBM), whole(pltpu.HBM)),
        scratch_shapes=[
            pltpu.SMEM(send_count.shape, jnp.int32),
            VMEM((PARTS, SLAB, channels // PARTS), f32),
            VMEM((1, SLAB), jnp.int32),
            VMEM(feed_gain.shape, f32),
            VMEM((3 * 32, channels), f32),
            VMEM((BAND, CAP), jnp.int32),
            VMEM((1, slots), jnp.int32),
            VMEM(unit, f32),
            VMEM(packed, f32),
            pltpu.SemaphoreType.DMA((6 + PARTS,)),
            pltpu.SemaphoreType.DMA((2 + PARTS,)),
        ],
        compiler_params=pltpu.CompilerParams(vmem_limit_bytes=VMEM_PREPARE << 20),
        name="prepare",
    )(
        send_count,
        spectra,
        feed_ids.reshape(1, SLAB),
        feed_gain,
        send_list,
        kernel_weight.T,
        pixel_block.reshape(1, slots),
    )


def grid_kernel(
    below2, below1, here, above1, above2, sums, packed_even, packed_odd, out,
    left_high, left_low, right, dense, tiles, done,
):
    for tile, pack in enumerate((packed_even, packed_odd)):
        weight = pack[0:KB, :]
        block = pack[KB : KB + 1, :]
        for number in range(PIX // KB):
            high, low = split(jnp.where(block == number, weight, 0.0))
            dense[tile, number * KB : (number + 1) * KB, :] = high
            dense[tile, PIX + number * KB : PIX + (number + 1) * KB, :] = low
    first, second = pl.ds(0, UNIT), pl.ds(UNIT, UNIT)
    slabs = [
        here.at[first],
        here.at[second],
        below1.at[first],
        below1.at[second],
        above1.at[first],
        above1.at[second],
        below2,
        above2.at[first],
        above2.at[second],
    ]
    places = [3, 4, 1, 2, 5, 6, 0, 7, 8]
    totals = [jnp.zeros((1, PIX), f32) for _ in range(CORES)]
    sample = lax.broadcasted_iota(jnp.int32, (SLAB, SLAB), 0).astype(f32)
    lane = lax.broadcasted_iota(jnp.int32, (SLAB, SLAB), 1)
    for index, unit in zip(places, slabs):
        scale = CH / sums[index : index + 1, :]
        high, low = split(unit[0:HALF_CH, :] * scale)
        at = index * SLAB
        left_high[:, at : at + SLAB] = high
        left_low[:, at : at + SLAB] = low
        for tile in range(CORES):
            offset = tile + BAND - 1 - index
            if not 0 <= offset < BAND:
                continue
            pair = offset // 2
            chosen = unit[HALF_CH + pair : HALF_CH + pair + 1, :]
            hot = ((sample == chosen) & ((lane // CAP) == offset % 2)).astype(f32).astype(bf16)
            picked = lax.dot_general(
                hot,
                dense[tile, :, pair * SLAB : (pair + 1) * SLAB],
                (((1,), (1,)), ((), ())),
                preferred_element_type=f32,
            )
            totals[tile] = totals[tile] + jnp.sum(
                picked[:, 0:PIX] + picked[:, PIX:], axis=0, keepdims=True
            )
            start = (index - tile) * SLAB
            right[tile, start : start + SLAB, :] = picked.astype(bf16)
    copies = []
    for tile in range(CORES):
        span = slice(tile * SLAB, (tile + BAND) * SLAB)
        both = jnp.dot(left_high[:, span], right[tile], preferred_element_type=f32)
        rest = jnp.dot(left_low[:, span], right[tile, :, 0:PIX], preferred_element_type=f32)
        gridded = (both[:, 0:PIX] + both[:, PIX:] + rest) / jnp.maximum(totals[tile], 1.0)
        for row in range(TY):
            out[:, tile * TY + row] = gridded[:, row * TX : (row + 1) * TX].reshape(
                HALF_CH // 8, 8, TX
            )


def grid_tiles(units, sums, packed_even, packed_odd):
    slots = BAND * CAP
    depth = REACH * SLAB
    return pl.pallas_call(
        grid_kernel,
        out_shape=jax.ShapeDtypeStruct((HALF_CH // 8, CORES * TY, 8, TX), f32),
        in_specs=[whole()] * 8,
        out_specs=whole(),
        scratch_shapes=[
            VMEM((HALF_CH, depth), bf16),
            VMEM((HALF_CH, depth), bf16),
            VMEM((CORES, BAND * SLAB, 2 * PIX), bf16),
            VMEM((CORES, 2 * PIX, slots), bf16),
            VMEM((CORES, HALF_CH // 8, TY, 8, TX), f32),
            pltpu.SemaphoreType.DMA((CORES,)),
        ],
        compiler_params=pltpu.CompilerParams(vmem_limit_bytes=32 << 20),
        name="grid_tiles",
    )(*units, sums, packed_even, packed_odd)


def waves(length):
    frequency = jnp.arange(length, dtype=jnp.int32)
    phases = (frequency[:, None] * frequency[None, :] % length).astype(f32) * (
        2.0 * math.pi / length
    )
    return jnp.concatenate([jnp.cos(phases), jnp.sin(phases)], axis=1)


def response(sigma, length):
    frequency = lax.broadcasted_iota(jnp.int32, (1, 2 * length), 1) % length
    folded = jnp.minimum(frequency, length - frequency).astype(f32) / length
    return jnp.exp(-2.0 * math.pi**2 * sigma**2 * folded**2)


def circulant(sigma, basis, rows):
    length = basis.shape[0]
    return (
        lax.dot_general(
            basis[0:rows] * response(sigma, length),
            basis,
            (((1,), (1,)), ((), ())),
            precision=highest,
            preferred_element_type=f32,
        )
        / length
    )


def tables_kernel(sigma, row_waves, column_waves, rows_out, columns_out):
    width = sigma[pl.program_id(0)]
    half = rows_out.shape[2]
    high, low = split(circulant(width, row_waves[...], half))
    rows_out[0, 0] = high
    rows_out[0, 1] = low
    high, low = split(circulant(width, column_waves[...], TX))
    columns_out[0, :, 0:TX] = high
    columns_out[0, :, TX:] = low


def make_tables(sigma, length):
    channels = sigma.shape[0]
    waves_rows = waves(length)
    fixed = lambda shape: pl.BlockSpec(shape, lambda c: (0, 0))
    return pl.pallas_call(
        tables_kernel,
        grid=(channels,),
        out_shape=(
            jax.ShapeDtypeStruct((channels, 2, length // 2, length), bf16),
            jax.ShapeDtypeStruct((channels, TX, 2 * TX), bf16),
        ),
        in_specs=[
            whole(pltpu.SMEM),
            fixed((length, 2 * length)),
            fixed((TX, 2 * TX)),
        ],
        out_specs=(
            pl.BlockSpec((1, 2, length // 2, length), lambda c: (c, 0, 0, 0)),
            pl.BlockSpec((1, TX, 2 * TX), lambda c: (c, 0, 0)),
        ),
        compiler_params=pltpu.CompilerParams(vmem_limit_bytes=60 << 20),
        cost_estimate=pl.CostEstimate(
            flops=2 * channels * 6 * 2 * length**3, bytes_accessed=6 << 20, transcendentals=0
        ),
        name="smoothing_tables",
    )(sigma, waves_rows, waves(TX))


def smooth_kernel(
    field, rows_in, columns_in, out, rows_table, columns_table, across, smoothed, here, done
):
    channels, length, _ = smoothed.shape
    half = length // 2
    columns_copy = pltpu.make_async_copy(columns_in, columns_table, here.at[0])
    rows_copy = pltpu.make_async_copy(rows_in, rows_table, here.at[1])
    columns_copy.start()
    rows_copy.start()
    for c in range(channels):
        high, low = split(field[pl.ds(c, length, stride=channels), :])
        across[c, :, 0:TX] = high
        across[c, :, TX:] = low
    columns_copy.wait()
    none = jnp.zeros((TX, TX), bf16)
    for c in range(channels):
        table = columns_table[c]
        table = jnp.concatenate(
            [table, jnp.concatenate([table[:, 0:TX], none], axis=1)], axis=0
        )
        both = jnp.dot(across[c], table, preferred_element_type=f32)
        high, low = split(both[:, 0:TX] + both[:, TX:])
        across[c, :, 0:TX] = high
        across[c, :, TX:] = low
    rows_copy.wait()
    group = channels // GROUPS
    copies = []
    for number in range(GROUPS):
        for c in range(number * group, (number + 1) * group):
            straight = across[c]
            swapped = jnp.concatenate([straight[half:], straight[:half]], axis=0)
            highs = jnp.concatenate([straight[:, 0:TX], swapped[:, 0:TX]], axis=1)
            lows = jnp.concatenate([straight[:, TX:], swapped[:, TX:]], axis=1)
            total = jnp.dot(rows_table[c, 0], highs, preferred_element_type=f32)
            total = total + jnp.dot(rows_table[c, 0], lows, preferred_element_type=f32)
            total = total + jnp.dot(rows_table[c, 1], highs, preferred_element_type=f32)
            smoothed[c, 0:half, :] = total[:, 0:TX]
            smoothed[c, half:, :] = total[:, TX:]
        part = pl.ds(number * group, group)
        copies.append(pltpu.make_async_copy(smoothed.at[part], out.at[part], done.at[number]))
        copies[-1].start()
    for copy in copies:
        copy.wait()


def smooth(field, rows_table, columns_table):
    channels, _, _, length = rows_table.shape
    return pl.pallas_call(
        smooth_kernel,
        out_shape=jax.ShapeDtypeStruct((channels, length, TX), f32),
        in_specs=[whole(), whole(pltpu.HBM), whole(pltpu.HBM)],
        out_specs=whole(pltpu.HBM),
        scratch_shapes=[
            VMEM(rows_table.shape, bf16),
            VMEM(columns_table.shape, bf16),
            VMEM((channels, length, 2 * TX), bf16),
            VMEM((channels, length, TX), f32),
            pltpu.SemaphoreType.DMA((2,)),
            pltpu.SemaphoreType.DMA((GROUPS,)),
        ],
        compiler_params=pltpu.CompilerParams(vmem_limit_bytes=VMEM_SMOOTH << 20),
        name="smooth",
    )(field, rows_table, columns_table)


def sum_rows(block):
    starts = range(HALF_CH + BAND // 2, block.shape[0], UNIT)
    return jnp.concatenate([block[start : start + 1] for start in starts], axis=0)


def local(
    spectra, feed_ids, feed_gain, send_list, send_count, kernel_weight, pixel_block, beam_width
):
    chips = lax.axis_size(("y", "z"))

    def shift(array, by):
        return lax.ppermute(array, ("y", "z"), [(i, (i + by) % chips) for i in range(chips)])

    unit, packed = prepare(
        spectra, feed_ids, feed_gain, send_list, send_count, kernel_weight, pixel_block
    )
    unit = unit.reshape(CORES * UNIT, SLAB)
    here = lax.all_to_all(unit, "core", split_axis=0, concat_axis=0, tiled=True)
    packed_other = lax.ppermute(packed, "core", [(0, 1), (1, 0)])
    above1, below1 = shift(here, -1), shift(here, 1)
    part_above2 = shift(sum_rows(here), -2)
    part_below2 = shift(sum_rows(here)[1:], 2)
    above2 = shift(above1, -1)
    below2 = shift(below1[UNIT:], 1)
    parts = [part_below2] + [sum_rows(block) for block in (below1, here, above1)] + [part_above2]
    sums = lax.psum(jnp.concatenate(parts, axis=0), "chan")
    even = lax.axis_index("core") == 0
    gridded = grid_tiles(
        (below2, below1, here, above1, above2),
        sums,
        jnp.where(even, packed, packed_other),
        jnp.where(even, packed_other, packed),
    )
    gridded, beam_width = lax.optimization_barrier((gridded, beam_width))
    relaid = lax.all_to_all(gridded, ("y", "z"), split_axis=0, concat_axis=0, tiled=True)
    rows_table, columns_table = make_tables(beam_width, chips * CORES * TY)
    return smooth(relaid.reshape(chips * CORES * TY * 8, TX), rows_table, columns_table)


def solution(mesh):
    tiles, channels = mesh.devices.shape
    chips = tiles // CORES
    grid = Mesh(
        mesh.devices.reshape(chips // ROWS_Z, ROWS_Z, CORES, channels), ("y", "z", "core", "chan")
    )
    tile = ("y", "z", "core")
    in_specs = (
        P(tile, "chan"),
        P(tile),
        P(None, "chan"),
        P(tile, None),
        P(tile),
        P(tile, None),
        P(tile),
        P(("chan",) + tile),
    )
    out_specs = P(("chan",) + tile, None, None)
    return jax.shard_map(local, mesh=grid, in_specs=in_specs, out_specs=out_specs, check_vma=False)
```

```python
import math

import jax
import jax.numpy as jnp
from jax import lax
from jax.experimental import pallas as pl
from jax.experimental.pallas import tpu as pltpu
from jax.sharding import Mesh
from jax.sharding import PartitionSpec as P

CH = 4096
TY = 2
TX = 128
CORES = 2
ROWS_Z = 16
SLAB = 128
BAND = 8
CAP = 64
KB = 64
HALF_CH = 512
META = 8
UNIT = HALF_CH + META
REACH = 9
GROUPS = 8
PARTS = 4
VMEM_SMOOTH = 105
VMEM_PREPARE = 56
PIX = TY * TX

f32 = jnp.float32
bf16 = jnp.bfloat16
highest = lax.Precision.HIGHEST
VMEM = pltpu.VMEM


def whole(memory_space=VMEM):
    return pl.BlockSpec(memory_space=memory_space)


def split(value):
    high = value.astype(bf16)
    return high, (value - high.astype(f32)).astype(bf16)


def prepare_kernel(
    counts_in,
    spectra_in,
    feed_ids_in,
    feed_gain_in,
    send_list_in,
    weights_in,
    blocks_in,
    unit_out,
    packed_out,
    counts,
    spectra,
    feed_ids,
    feed_gain,
    gains,
    send_list,
    blocks,
    unit,
    packed,
    arrived,
    left,
):
    feeds, channels = feed_gain.shape
    width = channels // PARTS
    rows = HALF_CH // PARTS
    room = gains.shape[0] // 3
    copies = []

    def fetch(source, target):
        copies.append(pltpu.make_async_copy(source, target, arrived.at[len(copies)]))
        copies[-1].start()

    fetch(feed_ids_in, feed_ids)
    fetch(feed_gain_in, feed_gain)
    for part in range(PARTS):
        columns = pl.ds(part * width, width)
        fetch(spectra_in.at[:, columns], spectra.at[part])
    fetch(send_list_in, send_list)
    fetch(blocks_in, blocks)
    fetch(weights_in, packed.at[0:KB])
    fetch(counts_in, counts)
    gains[...] = jnp.zeros_like(gains)
    copies[0].wait()
    copies[1].wait()
    value = feed_gain[...]
    for step in range(3):
        piece = value.astype(bf16)
        value = value - piece.astype(f32)
        gains[step * room : step * room + feeds, :] = piece.astype(f32)
    onehot = (
        lax.broadcasted_iota(jnp.int32, (3 * room, SLAB), 0) % room == feed_ids[...]
    ).astype(f32)
    onehot = onehot.astype(bf16)
    band_sum = jnp.zeros((1, SLAB), f32)
    sends = []

    def send(source, target):
        sends.append(pltpu.make_async_copy(source, target, left.at[len(sends)]))
        sends[-1].start()

    for part in range(PARTS):
        gain_rows = lax.dot_general(
            gains[:, part * width : (part + 1) * width].astype(bf16),
            onehot,
            (((0,), (0,)), ((), ())),
            preferred_element_type=f32,
        )
        copies[2 + part].wait()
        raw = spectra[part].T
        band_sum = band_sum + jnp.sum(raw, axis=0, keepdims=True)
        scaled = (raw * gain_rows).reshape(rows // 8, CORES, 8, SLAB)
        for core in range(CORES):
            unit[core, part * rows : (part + 1) * rows, :] = scaled[:, core].reshape(rows, SLAB)
        span = pl.ds(part * rows, rows)
        send(unit.at[:, span], unit_out.at[:, span])
    copies[2 + PARTS].wait()
    copies[5 + PARTS].wait()
    lane = lax.broadcasted_iota(jnp.int32, (1, CAP), 1)
    lists = [
        jnp.where(lane < counts[row], send_list[row : row + 1, :], -1).astype(f32)
        for row in range(BAND)
    ]
    lists = [jnp.concatenate(lists[2 * m : 2 * m + 2], axis=1) for m in range(BAND // 2)]
    meta = jnp.concatenate(lists + [band_sum, jnp.zeros((META - BAND // 2 - 1, SLAB), f32)], axis=0)
    for core in range(CORES):
        unit[core, HALF_CH:UNIT, :] = meta
    span = pl.ds(HALF_CH, META)
    send(unit.at[:, span], unit_out.at[:, span])
    copies[3 + PARTS].wait()
    packed[KB : KB + 8, :] = jnp.broadcast_to(blocks[...].astype(f32), (8, BAND * CAP))
    copies[4 + PARTS].wait()
    send(packed, packed_out)
    for copy in sends:
        copy.wait()


def prepare(spectra, feed_ids, feed_gain, send_list, send_count, kernel_weight, pixel_block):
    slots = BAND * CAP
    channels = spectra.shape[1]
    unit = (CORES, UNIT, SLAB)
    packed = (KB + 8, slots)
    return pl.pallas_call(
        prepare_kernel,
        out_shape=(jax.ShapeDtypeStruct(unit, f32), jax.ShapeDtypeStruct(packed, f32)),
        in_specs=[whole(pltpu.HBM)] * 7,
        out_specs=(whole(pltpu.HBM), whole(pltpu.HBM)),
        scratch_shapes=[
            pltpu.SMEM(send_count.shape, jnp.int32),
            VMEM((PARTS, SLAB, channels // PARTS), f32),
            VMEM((1, SLAB), jnp.int32),
            VMEM(feed_gain.shape, f32),
            VMEM((3 * 32, channels), f32),
            VMEM((BAND, CAP), jnp.int32),
            VMEM((1, slots), jnp.int32),
            VMEM(unit, f32),
            VMEM(packed, f32),
            pltpu.SemaphoreType.DMA((6 + PARTS,)),
            pltpu.SemaphoreType.DMA((2 + PARTS,)),
        ],
        compiler_params=pltpu.CompilerParams(vmem_limit_bytes=VMEM_PREPARE << 20),
        name="prepare",
    )(
        send_count,
        spectra,
        feed_ids.reshape(1, SLAB),
        feed_gain,
        send_list,
        kernel_weight.T,
        pixel_block.reshape(1, slots),
    )


def grid_kernel(
    below2, below1, here, above1, above2, sums, packed_even, packed_odd, out,
    left_high, left_low, right, dense, tiles, done,
):
    for tile, pack in enumerate((packed_even, packed_odd)):
        weight = pack[0:KB, :]
        block = pack[KB : KB + 1, :]
        for number in range(PIX // KB):
            high, low = split(jnp.where(block == number, weight, 0.0))
            dense[tile, number * KB : (number + 1) * KB, :] = high
            dense[tile, PIX + number * KB : PIX + (number + 1) * KB, :] = low
    first, second = pl.ds(0, UNIT), pl.ds(UNIT, UNIT)
    slabs = [
        here.at[first],
        here.at[second],
        below1.at[first],
        below1.at[second],
        above1.at[first],
        above1.at[second],
        below2,
        above2.at[first],
        above2.at[second],
    ]
    places = [3, 4, 1, 2, 5, 6, 0, 7, 8]
    totals = [jnp.zeros((1, PIX), f32) for _ in range(CORES)]
    sample = lax.broadcasted_iota(jnp.int32, (SLAB, SLAB), 0).astype(f32)
    lane = lax.broadcasted_iota(jnp.int32, (SLAB, SLAB), 1)
    for index, unit in zip(places, slabs):
        scale = CH / sums[index : index + 1, :]
        high, low = split(unit[0:HALF_CH, :] * scale)
        at = index * SLAB
        left_high[:, at : at + SLAB] = high
        left_low[:, at : at + SLAB] = low
        for tile in range(CORES):
            offset = tile + BAND - 1 - index
            if not 0 <= offset < BAND:
                continue
            pair = offset // 2
            chosen = unit[HALF_CH + pair : HALF_CH + pair + 1, :]
            hot = ((sample == chosen) & ((lane // CAP) == offset % 2)).astype(f32).astype(bf16)
            picked = lax.dot_general(
                hot,
                dense[tile, :, pair * SLAB : (pair + 1) * SLAB],
                (((1,), (1,)), ((), ())),
                preferred_element_type=f32,
            )
            totals[tile] = totals[tile] + jnp.sum(
                picked[:, 0:PIX] + picked[:, PIX:], axis=0, keepdims=True
            )
            start = (index - tile) * SLAB
            right[tile, start : start + SLAB, :] = picked.astype(bf16)
    copies = []
    for tile in range(CORES):
        span = slice(tile * SLAB, (tile + BAND) * SLAB)
        both = jnp.dot(left_high[:, span], right[tile], preferred_element_type=f32)
        rest = jnp.dot(left_low[:, span], right[tile, :, 0:PIX], preferred_element_type=f32)
        gridded = (both[:, 0:PIX] + both[:, PIX:] + rest) / jnp.maximum(totals[tile], 1.0)
        for row in range(TY):
            out[:, tile * TY + row] = gridded[:, row * TX : (row + 1) * TX].reshape(
                HALF_CH // 8, 8, TX
            )


def grid_tiles(units, sums, packed_even, packed_odd):
    slots = BAND * CAP
    depth = REACH * SLAB
    return pl.pallas_call(
        grid_kernel,
        out_shape=jax.ShapeDtypeStruct((HALF_CH // 8, CORES * TY, 8, TX), f32),
        in_specs=[whole()] * 8,
        out_specs=whole(),
        scratch_shapes=[
            VMEM((HALF_CH, depth), bf16),
            VMEM((HALF_CH, depth), bf16),
            VMEM((CORES, BAND * SLAB, 2 * PIX), bf16),
            VMEM((CORES, 2 * PIX, slots), bf16),
            VMEM((CORES, HALF_CH // 8, TY, 8, TX), f32),
            pltpu.SemaphoreType.DMA((CORES,)),
        ],
        compiler_params=pltpu.CompilerParams(vmem_limit_bytes=32 << 20),
        name="grid_tiles",
    )(*units, sums, packed_even, packed_odd)


def waves(length):
    frequency = jnp.arange(length, dtype=jnp.int32)
    phases = (frequency[:, None] * frequency[None, :] % length).astype(f32) * (
        2.0 * math.pi / length
    )
    return jnp.concatenate([jnp.cos(phases), jnp.sin(phases)], axis=1)


def response(sigma, length):
    frequency = lax.broadcasted_iota(jnp.int32, (1, 2 * length), 1) % length
    folded = jnp.minimum(frequency, length - frequency).astype(f32) / length
    return jnp.exp(-2.0 * math.pi**2 * sigma**2 * folded**2)


def circulant(sigma, basis, rows):
    length = basis.shape[0]
    return (
        lax.dot_general(
            basis[0:rows] * response(sigma, length),
            basis,
            (((1,), (1,)), ((), ())),
            precision=highest,
            preferred_element_type=f32,
        )
        / length
    )


def tables_kernel(sigma, row_waves, column_waves, tables_out):
    width = sigma[pl.program_id(0)]
    half = row_waves.shape[0] // 2
    high, low = split(circulant(width, row_waves[...], half))
    tables_out[0, 0:half] = high
    tables_out[0, half : 2 * half] = low
    high, low = split(circulant(width, column_waves[...], TX))
    tables_out[0, 2 * half :, 0:TX] = high
    tables_out[0, 2 * half :, TX:] = low


def make_tables(sigma, length):
    channels = sigma.shape[0]
    waves_rows = waves(length)
    fixed = lambda shape: pl.BlockSpec(shape, lambda c: (0, 0))
    return pl.pallas_call(
        tables_kernel,
        grid=(channels,),
        out_shape=jax.ShapeDtypeStruct((channels, length + TX, 2 * TX), bf16),
        in_specs=[
            whole(pltpu.SMEM),
            fixed((length, 2 * length)),
            fixed((TX, 2 * TX)),
        ],
        out_specs=pl.BlockSpec((1, length + TX, 2 * TX), lambda c: (c, 0, 0)),
        compiler_params=pltpu.CompilerParams(vmem_limit_bytes=60 << 20),
        cost_estimate=pl.CostEstimate(
            flops=2 * channels * 6 * 2 * length**3, bytes_accessed=6 << 20, transcendentals=0
        ),
        name="smoothing_tables",
    )(sigma, waves_rows, waves(TX))


def smooth_kernel(field, tables_in, out, tables, across, smoothed, here, done):
    channels, length, _ = smoothed.shape
    half = length // 2
    rows_part, columns_part = pl.ds(0, length), pl.ds(length, TX)
    columns_copy = pltpu.make_async_copy(
        tables_in.at[:, columns_part], tables.at[:, columns_part], here.at[0]
    )
    rows_copy = pltpu.make_async_copy(
        tables_in.at[:, rows_part], tables.at[:, rows_part], here.at[1]
    )
    columns_copy.start()
    rows_copy.start()
    for c in range(channels):
        high, low = split(field[pl.ds(c, length, stride=channels), :])
        across[c, :, 0:TX] = high
        across[c, :, TX:] = low
    columns_copy.wait()
    none = jnp.zeros((TX, TX), bf16)
    for c in range(channels):
        table = tables[c, length:, :]
        table = jnp.concatenate(
            [table, jnp.concatenate([table[:, 0:TX], none], axis=1)], axis=0
        )
        both = jnp.dot(across[c], table, preferred_element_type=f32)
        high, low = split(both[:, 0:TX] + both[:, TX:])
        across[c, :, 0:TX] = high
        across[c, :, TX:] = low
    rows_copy.wait()
    group = channels // GROUPS
    copies = []
    for number in range(GROUPS):
        for c in range(number * group, (number + 1) * group):
            straight = across[c]
            swapped = jnp.concatenate([straight[half:], straight[:half]], axis=0)
            highs = jnp.concatenate([straight[:, 0:TX], swapped[:, 0:TX]], axis=1)
            lows = jnp.concatenate([straight[:, TX:], swapped[:, TX:]], axis=1)
            total = jnp.dot(tables[c, 0:half, :], highs, preferred_element_type=f32)
            total = total + jnp.dot(tables[c, 0:half, :], lows, preferred_element_type=f32)
            total = total + jnp.dot(tables[c, half:length, :], highs, preferred_element_type=f32)
            smoothed[c, 0:half, :] = total[:, 0:TX]
            smoothed[c, half:, :] = total[:, TX:]
        part = pl.ds(number * group, group)
        copies.append(pltpu.make_async_copy(smoothed.at[part], out.at[part], done.at[number]))
        copies[-1].start()
    for copy in copies:
        copy.wait()


def smooth(field, tables):
    channels, rows, _ = tables.shape
    length = rows - TX
    return pl.pallas_call(
        smooth_kernel,
        out_shape=jax.ShapeDtypeStruct((channels, length, TX), f32),
        in_specs=[whole(), whole(pltpu.HBM)],
        out_specs=whole(pltpu.HBM),
        scratch_shapes=[
            VMEM(tables.shape, bf16),
            VMEM((channels, length, 2 * TX), bf16),
            VMEM((channels, length, TX), f32),
            pltpu.SemaphoreType.DMA((2,)),
            pltpu.SemaphoreType.DMA((GROUPS,)),
        ],
        compiler_params=pltpu.CompilerParams(vmem_limit_bytes=VMEM_SMOOTH << 19),
        name="smooth",
    )(field, tables)


def sum_rows(block):
    starts = range(HALF_CH + BAND // 2, block.shape[0], UNIT)
    return jnp.concatenate([block[start : start + 1] for start in starts], axis=0)


def local(
    spectra, feed_ids, feed_gain, send_list, send_count, kernel_weight, pixel_block, beam_width
):
    chips = lax.axis_size(("y", "z"))

    def shift(array, by):
        return lax.ppermute(array, ("y", "z"), [(i, (i + by) % chips) for i in range(chips)])

    unit, packed = prepare(
        spectra, feed_ids, feed_gain, send_list, send_count, kernel_weight, pixel_block
    )
    unit = unit.reshape(CORES * UNIT, SLAB)
    here = lax.all_to_all(unit, "core", split_axis=0, concat_axis=0, tiled=True)
    packed_other = lax.ppermute(packed, "core", [(0, 1), (1, 0)])
    above1, below1 = shift(here, -1), shift(here, 1)
    part_above2 = shift(sum_rows(here), -2)
    part_below2 = shift(sum_rows(here)[1:], 2)
    above2 = shift(above1, -1)
    below2 = shift(below1[UNIT:], 1)
    parts = [part_below2] + [sum_rows(block) for block in (below1, here, above1)] + [part_above2]
    sums = lax.psum(jnp.concatenate(parts, axis=0), "chan")
    even = lax.axis_index("core") == 0
    gridded = grid_tiles(
        (below2, below1, here, above1, above2),
        sums,
        jnp.where(even, packed, packed_other),
        jnp.where(even, packed_other, packed),
    )
    gridded, beam_width = lax.optimization_barrier((gridded, beam_width))
    relaid = lax.all_to_all(gridded, ("y", "z"), split_axis=0, concat_axis=0, tiled=True)
    tables = make_tables(beam_width, chips * CORES * TY)
    return smooth(relaid.reshape(chips * CORES * TY * 8, TX), tables)


def solution(mesh):
    tiles, channels = mesh.devices.shape
    chips = tiles // CORES
    grid = Mesh(
        mesh.devices.reshape(chips // ROWS_Z, ROWS_Z, CORES, channels), ("y", "z", "core", "chan")
    )
    tile = ("y", "z", "core")
    in_specs = (
        P(tile, "chan"),
        P(tile),
        P(None, "chan"),
        P(tile, None),
        P(tile),
        P(tile, None),
        P(tile),
        P(("chan",) + tile),
    )
    out_specs = P(("chan",) + tile, None, None)
    return jax.shard_map(local, mesh=grid, in_specs=in_specs, out_specs=out_specs, check_vma=False)
```

```python
import math

import jax
import jax.numpy as jnp
from jax import lax
from jax.experimental import pallas as pl
from jax.experimental.pallas import tpu as pltpu
from jax.sharding import Mesh
from jax.sharding import PartitionSpec as P

CH = 4096
TY = 2
TX = 128
CORES = 2
ROWS_Z = 16
SLAB = 128
BAND = 8
CAP = 64
KB = 64
HALF_CH = 512
META = 8
UNIT = HALF_CH + META
REACH = 9
GROUPS = 8
PARTS = 4
VMEM_SMOOTH = 105
VMEM_PREPARE = 56
PIX = TY * TX

f32 = jnp.float32
bf16 = jnp.bfloat16
highest = lax.Precision.HIGHEST
VMEM = pltpu.VMEM


def whole(memory_space=VMEM):
    return pl.BlockSpec(memory_space=memory_space)


def split(value):
    high = value.astype(bf16)
    return high, (value - high.astype(f32)).astype(bf16)


def prepare_kernel(
    counts_in,
    spectra_in,
    feed_ids_in,
    feed_gain_in,
    send_list_in,
    weights_in,
    blocks_in,
    unit_out,
    packed_out,
    counts,
    spectra,
    feed_ids,
    feed_gain,
    gains,
    send_list,
    blocks,
    unit,
    packed,
    arrived,
    left,
):
    feeds, channels = feed_gain.shape
    width = channels // PARTS
    rows = HALF_CH // PARTS
    room = gains.shape[0] // 3
    copies = []

    def fetch(source, target):
        copies.append(pltpu.make_async_copy(source, target, arrived.at[len(copies)]))
        copies[-1].start()

    fetch(feed_ids_in, feed_ids)
    fetch(feed_gain_in, feed_gain)
    for part in range(PARTS):
        columns = pl.ds(part * width, width)
        fetch(spectra_in.at[:, columns], spectra.at[part])
    fetch(send_list_in, send_list)
    fetch(blocks_in, blocks)
    fetch(weights_in, packed.at[0:KB])
    fetch(counts_in, counts)
    gains[...] = jnp.zeros_like(gains)
    copies[0].wait()
    copies[1].wait()
    value = feed_gain[...]
    for step in range(3):
        piece = value.astype(bf16)
        value = value - piece.astype(f32)
        gains[step * room : step * room + feeds, :] = piece.astype(f32)
    onehot = (
        lax.broadcasted_iota(jnp.int32, (3 * room, SLAB), 0) % room == feed_ids[...]
    ).astype(f32)
    onehot = onehot.astype(bf16)
    band_sum = jnp.zeros((1, SLAB), f32)
    sends = []

    def send(source, target):
        sends.append(pltpu.make_async_copy(source, target, left.at[len(sends)]))
        sends[-1].start()

    for part in range(PARTS):
        gain_rows = lax.dot_general(
            gains[:, part * width : (part + 1) * width].astype(bf16),
            onehot,
            (((0,), (0,)), ((), ())),
            preferred_element_type=f32,
        )
        copies[2 + part].wait()
        raw = spectra[part].T
        band_sum = band_sum + jnp.sum(raw, axis=0, keepdims=True)
        scaled = (raw * gain_rows).reshape(rows // 8, CORES, 8, SLAB)
        for core in range(CORES):
            unit[core, part * rows : (part + 1) * rows, :] = scaled[:, core].reshape(rows, SLAB)
        span = pl.ds(part * rows, rows)
        send(unit.at[:, span], unit_out.at[:, span])
    copies[2 + PARTS].wait()
    copies[5 + PARTS].wait()
    lane = lax.broadcasted_iota(jnp.int32, (1, CAP), 1)
    lists = [
        jnp.where(lane < counts[row], send_list[row : row + 1, :], -1).astype(f32)
        for row in range(BAND)
    ]
    lists = [jnp.concatenate(lists[2 * m : 2 * m + 2], axis=1) for m in range(BAND // 2)]
    meta = jnp.concatenate(lists + [band_sum, jnp.zeros((META - BAND // 2 - 1, SLAB), f32)], axis=0)
    for core in range(CORES):
        unit[core, HALF_CH:UNIT, :] = meta
    span = pl.ds(HALF_CH, META)
    send(unit.at[:, span], unit_out.at[:, span])
    copies[3 + PARTS].wait()
    packed[KB : KB + 8, :] = jnp.broadcast_to(blocks[...].astype(f32), (8, BAND * CAP))
    copies[4 + PARTS].wait()
    send(packed, packed_out)
    for copy in sends:
        copy.wait()


def prepare(spectra, feed_ids, feed_gain, send_list, send_count, kernel_weight, pixel_block):
    slots = BAND * CAP
    channels = spectra.shape[1]
    unit = (CORES, UNIT, SLAB)
    packed = (KB + 8, slots)
    return pl.pallas_call(
        prepare_kernel,
        out_shape=(jax.ShapeDtypeStruct(unit, f32), jax.ShapeDtypeStruct(packed, f32)),
        in_specs=[whole(pltpu.HBM)] * 7,
        out_specs=(whole(pltpu.HBM), whole(pltpu.HBM)),
        scratch_shapes=[
            pltpu.SMEM(send_count.shape, jnp.int32),
            VMEM((PARTS, SLAB, channels // PARTS), f32),
            VMEM((1, SLAB), jnp.int32),
            VMEM(feed_gain.shape, f32),
            VMEM((3 * 32, channels), f32),
            VMEM((BAND, CAP), jnp.int32),
            VMEM((1, slots), jnp.int32),
            VMEM(unit, f32),
            VMEM(packed, f32),
            pltpu.SemaphoreType.DMA((6 + PARTS,)),
            pltpu.SemaphoreType.DMA((2 + PARTS,)),
        ],
        compiler_params=pltpu.CompilerParams(vmem_limit_bytes=VMEM_PREPARE << 20),
        name="prepare",
    )(
        send_count,
        spectra,
        feed_ids.reshape(1, SLAB),
        feed_gain,
        send_list,
        kernel_weight.T,
        pixel_block.reshape(1, slots),
    )


def grid_kernel(
    below2, below1, here, above1, above2, sums, packed_own, packed_other, out,
    left_high, left_low, right, dense, tiles, done,
):
    core = lax.axis_index("core")
    for tile, pack in ((core, packed_own), (1 - core, packed_other)):
        weight = pack[0:KB, :]
        block = pack[KB : KB + 1, :]
        for number in range(PIX // KB):
            high, low = split(jnp.where(block == number, weight, 0.0))
            dense[tile, number * KB : (number + 1) * KB, :] = high
            dense[tile, PIX + number * KB : PIX + (number + 1) * KB, :] = low
    first, second = pl.ds(0, UNIT), pl.ds(UNIT, UNIT)
    slabs = [
        here.at[first],
        here.at[second],
        below1.at[first],
        below1.at[second],
        above1.at[first],
        above1.at[second],
        below2,
        above2.at[first],
        above2.at[second],
    ]
    places = [3, 4, 1, 2, 5, 6, 0, 7, 8]
    totals = [jnp.zeros((1, PIX), f32) for _ in range(CORES)]
    sample = lax.broadcasted_iota(jnp.int32, (SLAB, SLAB), 0).astype(f32)
    lane = lax.broadcasted_iota(jnp.int32, (SLAB, SLAB), 1)
    for index, unit in zip(places, slabs):
        scale = CH / sums[index : index + 1, :]
        high, low = split(unit[0:HALF_CH, :] * scale)
        at = index * SLAB
        left_high[:, at : at + SLAB] = high
        left_low[:, at : at + SLAB] = low
        for tile in range(CORES):
            offset = tile + BAND - 1 - index
            if not 0 <= offset < BAND:
                continue
            pair = offset // 2
            chosen = unit[HALF_CH + pair : HALF_CH + pair + 1, :]
            hot = ((sample == chosen) & ((lane // CAP) == offset % 2)).astype(f32).astype(bf16)
            picked = lax.dot_general(
                hot,
                dense[tile, :, pair * SLAB : (pair + 1) * SLAB],
                (((1,), (1,)), ((), ())),
                preferred_element_type=f32,
            )
            totals[tile] = totals[tile] + jnp.sum(
                picked[:, 0:PIX] + picked[:, PIX:], axis=0, keepdims=True
            )
            start = (index - tile) * SLAB
            right[tile, start : start + SLAB, :] = picked.astype(bf16)
    copies = []
    for tile in range(CORES):
        span = slice(tile * SLAB, (tile + BAND) * SLAB)
        both = jnp.dot(left_high[:, span], right[tile], preferred_element_type=f32)
        rest = jnp.dot(left_low[:, span], right[tile, :, 0:PIX], preferred_element_type=f32)
        gridded = (both[:, 0:PIX] + both[:, PIX:] + rest) / jnp.maximum(totals[tile], 1.0)
        for row in range(TY):
            out[:, tile * TY + row] = gridded[:, row * TX : (row + 1) * TX].reshape(
                HALF_CH // 8, 8, TX
            )


def grid_tiles(units, sums, packed_own, packed_other):
    slots = BAND * CAP
    depth = REACH * SLAB
    return pl.pallas_call(
        grid_kernel,
        out_shape=jax.ShapeDtypeStruct((HALF_CH // 8, CORES * TY, 8, TX), f32),
        in_specs=[whole()] * 8,
        out_specs=whole(),
        scratch_shapes=[
            VMEM((HALF_CH, depth), bf16),
            VMEM((HALF_CH, depth), bf16),
            VMEM((CORES, BAND * SLAB, 2 * PIX), bf16),
            VMEM((CORES, 2 * PIX, slots), bf16),
            VMEM((CORES, HALF_CH // 8, TY, 8, TX), f32),
            pltpu.SemaphoreType.DMA((CORES,)),
        ],
        compiler_params=pltpu.CompilerParams(vmem_limit_bytes=32 << 20),
        name="grid_tiles",
    )(*units, sums, packed_own, packed_other)


def waves(length):
    frequency = jnp.arange(length, dtype=jnp.int32)
    phases = (frequency[:, None] * frequency[None, :] % length).astype(f32) * (
        2.0 * math.pi / length
    )
    return jnp.concatenate([jnp.cos(phases), jnp.sin(phases)], axis=1)


def response(sigma, length):
    frequency = lax.broadcasted_iota(jnp.int32, (1, 2 * length), 1) % length
    folded = jnp.minimum(frequency, length - frequency).astype(f32) / length
    return jnp.exp(-2.0 * math.pi**2 * sigma**2 * folded**2)


def circulant(sigma, basis, rows):
    length = basis.shape[0]
    return (
        lax.dot_general(
            basis[0:rows] * response(sigma, length),
            basis,
            (((1,), (1,)), ((), ())),
            precision=highest,
            preferred_element_type=f32,
        )
        / length
    )


def tables_kernel(sigma, row_waves, column_waves, tables_out):
    width = sigma[pl.program_id(0)]
    half = row_waves.shape[0] // 2
    high, low = split(circulant(width, row_waves[...], half))
    tables_out[0, 0:half] = high
    tables_out[0, half : 2 * half] = low
    high, low = split(circulant(width, column_waves[...], TX))
    tables_out[0, 2 * half :, 0:TX] = high
    tables_out[0, 2 * half :, TX:] = low


def make_tables(sigma, length):
    channels = sigma.shape[0]
    waves_rows = waves(length)
    fixed = lambda shape: pl.BlockSpec(shape, lambda c: (0, 0))
    return pl.pallas_call(
        tables_kernel,
        grid=(channels,),
        out_shape=jax.ShapeDtypeStruct((channels, length + TX, 2 * TX), bf16),
        in_specs=[
            whole(pltpu.SMEM),
            fixed((length, 2 * length)),
            fixed((TX, 2 * TX)),
        ],
        out_specs=pl.BlockSpec((1, length + TX, 2 * TX), lambda c: (c, 0, 0)),
        compiler_params=pltpu.CompilerParams(vmem_limit_bytes=60 << 20),
        cost_estimate=pl.CostEstimate(
            flops=2 * channels * 6 * 2 * length**3, bytes_accessed=6 << 20, transcendentals=0
        ),
        name="smoothing_tables",
    )(sigma, waves_rows, waves(TX))


def smooth_kernel(field, tables_in, out, tables, across, smoothed, here, done):
    channels, length, _ = smoothed.shape
    half = length // 2
    rows_part, columns_part = pl.ds(0, length), pl.ds(length, TX)
    columns_copy = pltpu.make_async_copy(
        tables_in.at[:, columns_part], tables.at[:, columns_part], here.at[0]
    )
    rows_copy = pltpu.make_async_copy(
        tables_in.at[:, rows_part], tables.at[:, rows_part], here.at[1]
    )
    columns_copy.start()
    rows_copy.start()
    for c in range(channels):
        high, low = split(field[pl.ds(c, length, stride=channels), :])
        across[c, :, 0:TX] = high
        across[c, :, TX:] = low
    columns_copy.wait()
    none = jnp.zeros((TX, TX), bf16)
    for c in range(channels):
        table = tables[c, length:, :]
        table = jnp.concatenate(
            [table, jnp.concatenate([table[:, 0:TX], none], axis=1)], axis=0
        )
        both = jnp.dot(across[c], table, preferred_element_type=f32)
        high, low = split(both[:, 0:TX] + both[:, TX:])
        across[c, :, 0:TX] = high
        across[c, :, TX:] = low
    rows_copy.wait()
    group = channels // GROUPS
    copies = []
    for number in range(GROUPS):
        for c in range(number * group, (number + 1) * group):
            straight = across[c]
            swapped = jnp.concatenate([straight[half:], straight[:half]], axis=0)
            highs = jnp.concatenate([straight[:, 0:TX], swapped[:, 0:TX]], axis=1)
            lows = jnp.concatenate([straight[:, TX:], swapped[:, TX:]], axis=1)
            total = jnp.dot(tables[c, 0:half, :], highs, preferred_element_type=f32)
            total = total + jnp.dot(tables[c, 0:half, :], lows, preferred_element_type=f32)
            total = total + jnp.dot(tables[c, half:length, :], highs, preferred_element_type=f32)
            smoothed[c, 0:half, :] = total[:, 0:TX]
            smoothed[c, half:, :] = total[:, TX:]
        part = pl.ds(number * group, group)
        copies.append(pltpu.make_async_copy(smoothed.at[part], out.at[part], done.at[number]))
        copies[-1].start()
    for copy in copies:
        copy.wait()


def smooth(field, tables):
    channels, rows, _ = tables.shape
    length = rows - TX
    return pl.pallas_call(
        smooth_kernel,
        out_shape=jax.ShapeDtypeStruct((channels, length, TX), f32),
        in_specs=[whole(), whole(pltpu.HBM)],
        out_specs=whole(pltpu.HBM),
        scratch_shapes=[
            VMEM(tables.shape, bf16),
            VMEM((channels, length, 2 * TX), bf16),
            VMEM((channels, length, TX), f32),
            pltpu.SemaphoreType.DMA((2,)),
            pltpu.SemaphoreType.DMA((GROUPS,)),
        ],
        compiler_params=pltpu.CompilerParams(vmem_limit_bytes=VMEM_SMOOTH << 19),
        name="smooth",
    )(field, tables)


def sum_rows(block):
    starts = range(HALF_CH + BAND // 2, block.shape[0], UNIT)
    return jnp.concatenate([block[start : start + 1] for start in starts], axis=0)


def local(
    spectra, feed_ids, feed_gain, send_list, send_count, kernel_weight, pixel_block, beam_width
):
    chips = lax.axis_size(("y", "z"))

    def shift(array, by):
        return lax.ppermute(array, ("y", "z"), [(i, (i + by) % chips) for i in range(chips)])

    unit, packed = prepare(
        spectra, feed_ids, feed_gain, send_list, send_count, kernel_weight, pixel_block
    )
    unit = unit.reshape(CORES * UNIT, SLAB)
    here = lax.all_to_all(unit, "core", split_axis=0, concat_axis=0, tiled=True)
    packed_other = lax.ppermute(packed, "core", [(0, 1), (1, 0)])
    above1, below1 = shift(here, -1), shift(here, 1)
    part_above2 = shift(sum_rows(here), -2)
    part_below2 = shift(sum_rows(here)[1:], 2)
    above2 = shift(above1, -1)
    below2 = shift(below1[UNIT:], 1)
    parts = [part_below2] + [sum_rows(block) for block in (below1, here, above1)] + [part_above2]
    sums = lax.psum(jnp.concatenate(parts, axis=0), "chan")
    gridded = grid_tiles(
        (below2, below1, here, above1, above2),
        sums,
        packed,
        packed_other,
    )
    gridded, beam_width = lax.optimization_barrier((gridded, beam_width))
    relaid = lax.all_to_all(gridded, ("y", "z"), split_axis=0, concat_axis=0, tiled=True)
    tables = make_tables(beam_width, chips * CORES * TY)
    return smooth(relaid.reshape(chips * CORES * TY * 8, TX), tables)


def solution(mesh):
    tiles, channels = mesh.devices.shape
    chips = tiles // CORES
    grid = Mesh(
        mesh.devices.reshape(chips // ROWS_Z, ROWS_Z, CORES, channels), ("y", "z", "core", "chan")
    )
    tile = ("y", "z", "core")
    in_specs = (
        P(tile, "chan"),
        P(tile),
        P(None, "chan"),
        P(tile, None),
        P(tile),
        P(tile, None),
        P(tile),
        P(("chan",) + tile),
    )
    out_specs = P(("chan",) + tile, None, None)
    return jax.shard_map(local, mesh=grid, in_specs=in_specs, out_specs=out_specs, check_vma=False)
```
